512 devices in a mesh: blk: 32 (over x, z_lo), rep: 16 (over z_hi, y, core).
Axes of the slice: x: 4, y: 4, z: 16 (z_hi: 2, z_lo: 8; z = z_hi * 8 + z_lo), core: 2. Of those that a mesh axis runs over, the one named last changes fastest.
Arguments:
- features: bfloat16 [65536, 128], P(('blk', 'rep')), may hold values from -6 to 6
- weight: bfloat16 [128, 128], replicated, may hold values from -0.5 to 0.5
- adjacency: bfloat16 [32, 16, 2, 32, 2, 128, 128], P('blk', 'rep'), may hold values from 0 to 0.019042969
- row_tiles: int32 [32, 16, 2, 32, 2], P('blk', 'rep'), may hold values from 0 to 15
- live_counts: int32 [32, 16, 2, 32], P('blk', 'rep'), may hold values from 0 to 2, as said below
- upstream: bfloat16 [65536, 128], P(('blk', 'rep')), may hold values from -6 to 6
Outputs:
- hidden: bfloat16 [65536, 128], P(('blk', 'rep'))
- input_grad: bfloat16 [65536, 128], P(('blk', 'rep'))
- weight_grad: float32 [128, 128], replicated
The draws below stay inside these ranges and needn't reach their ends.
Inputs may be any that keep to these rules, and one draw needn't show every extreme that they name: `live_counts`: in every device's own set (s = 0) at least one bucket is full; row blocks differ in load, and a device's second set holds tiles of the row block before its own.
All inputs are finite; a program needn't handle non-finite values.
Results may differ from the reference program's by a relative error of at most 0.03.
Values may be sent and summed in bfloat16 or wider, within the bound.
A program may use at most 64 MiB of HBM per device.

```python
import jax
import jax.numpy as jnp
from jax import lax

F = 128
TILE = 128
SLOT = 2
BLOCKS = 32
REPS = 16
NODES = 65536


def draw_live_counts(key, part):
    key = jax.random.fold_in(key, 11)
    heat_key, base_key, full_key = jax.random.split(key, 3)
    heat = jax.random.randint(heat_key, (BLOCKS,), 0, 4)
    level = jnp.stack([heat, jnp.roll(heat, 1)], axis=1)
    base = jax.random.randint(base_key, (BLOCKS, REPS, 2, BLOCKS), 0, SLOT + 1)
    counts = base * (1 + level[:, None, :, None]) // 4
    full_column = jax.random.randint(full_key, (BLOCKS, REPS, 1, 1), 0, BLOCKS)
    column_ids = jnp.arange(BLOCKS, dtype=jnp.int32)[None, None, None, :]
    set_ids = jnp.arange(2, dtype=jnp.int32)[None, None, :, None]
    counts = jnp.where((column_ids == full_column) & (set_ids == 0), SLOT, counts)
    return counts.astype(jnp.int32)


def place_ends(entries, rng, smallest, largest):
    dims = entries.shape
    place = [jax.random.randint(jax.random.fold_in(rng, axis), (), 0, dims[axis]) for axis in range(len(dims))]
    entries = entries.at[tuple(place)].set(smallest)
    longest = dims.index(max(dims))
    place[longest] = (place[longest] + 1) % dims[longest]
    return entries.at[tuple(place)].set(largest)


def level_of(own_key, extent, shards, low, largest):
    def one(axis_at, blocks):
        heights = jax.random.uniform(jax.random.fold_in(jax.random.fold_in(own_key, 6), axis_at), (blocks,), jnp.float32, low / len(shards), largest / len(shards))
        return jnp.repeat(jnp.exp(heights), extent[axis_at] // blocks).reshape((-1,) + (1,) * (len(extent) - axis_at - 1))

    level = one(*shards[0])
    for cut in shards[1:]:
        level = level * one(*cut)
    return level


def noise(key, dims, scale, bound, cuts=(), held_as=jnp.bfloat16):
    entries = jax.random.normal(key, dims, jnp.float32) * scale
    if len(cuts) > 0:
        entries = level_of(key, dims, cuts, -0.22, 0.18) * entries
    return jnp.clip(entries, min=-bound, max=bound).astype(held_as)


def setup_inputs(seed: int = 0) -> dict:
    key_list = jax.random.split(jax.random.key(seed), 7)
    features = noise(key_list[0], (NODES, F), 1.0, 6.0, ((0, 512),))
    weight = noise(key_list[1], (F, F), F ** -0.5, 0.5)
    adjacency = jnp.clip(0.019042969 * jax.random.uniform(key_list[2], (BLOCKS, REPS, 2, BLOCKS, SLOT, TILE, TILE), jnp.float32) ** level_of(key_list[2], (BLOCKS, REPS, 2, BLOCKS, SLOT, TILE, TILE), ((0, 32), (1, 16)), -0.2, 0.2), 0.0, 0.019042969).astype(jnp.bfloat16)
    row_tiles = place_ends(jax.random.randint(key_list[3], (BLOCKS, REPS, 2, BLOCKS, SLOT), 0, REPS), jax.random.fold_in(key_list[3], 1), 0, REPS - 1).astype(jnp.int32)
    live_counts = draw_live_counts(jax.random.fold_in(key_list[6], 71), 0)
    upstream = noise(key_list[5], (NODES, F), 1.0, 6.0, ((0, 512),))
    return {"features": features, "weight": weight, "adjacency": adjacency, "row_tiles": row_tiles, "live_counts": live_counts, "upstream": upstream}


def silu_slope(values):
    squashed = jax.nn.sigmoid(values)
    return squashed * (1.0 + values * (1.0 - squashed))


def reference(features, weight, adjacency, row_tiles, live_counts, upstream):
    tile_side = adjacency.shape[-1]
    width = features.shape[1]
    mixed = jnp.dot(features, weight, preferred_element_type=jnp.float32).astype(jnp.bfloat16)
    by_column = jnp.transpose(mixed.reshape(BLOCKS, REPS, tile_side, width), (1, 0, 2, 3)).astype(jnp.float32)
    alive_slots = jnp.arange(SLOT, dtype=jnp.int32) < live_counts[..., None]
    chooser = ((row_tiles[..., None] == jnp.arange(REPS, dtype=jnp.int32)) & alive_slots[..., None]).astype(jnp.float32)

    def forward_block(pair):
        owner_tiles, pick_table = pair
        products = jnp.einsum("rsckij,rcjf->rsckif", owner_tiles.astype(jnp.float32), by_column, precision=lax.Precision.HIGHEST)
        return jnp.einsum("rsckt,rsckif->stif", pick_table, products, precision=lax.Precision.HIGHEST)

    partials = lax.map(forward_block, (adjacency, chooser))
    owned = partials[:, 0].reshape(BLOCKS, REPS * tile_side, width)
    helped = partials[:, 1].reshape(BLOCKS, REPS * tile_side, width)
    summed = owned + jnp.roll(helped, -1, axis=0)
    hidden = jax.nn.silu(summed).astype(jnp.bfloat16)
    cotangent = upstream.reshape(BLOCKS, REPS * tile_side, width).astype(jnp.float32)
    slope = (cotangent * silu_slope(summed)).astype(jnp.bfloat16)
    slope_sets = jnp.stack([slope, jnp.roll(slope, 1, axis=0)], axis=1)
    slope_sets = slope_sets.reshape(BLOCKS, 2, REPS, tile_side, width).astype(jnp.float32)

    def backward_block(running, triple):
        owner_tiles, pick_table, chosen_sets = triple
        chosen = jnp.einsum("rsckt,stif->rsckif", pick_table, chosen_sets, precision=lax.Precision.HIGHEST)
        update = jnp.einsum("rsckij,rsckif->crjf", owner_tiles.astype(jnp.float32), chosen, precision=lax.Precision.HIGHEST)
        return running + update, None

    initial = jnp.zeros((BLOCKS, REPS, tile_side, width), jnp.float32)
    pulled_sum, unused = lax.scan(backward_block, initial, (adjacency, chooser, slope_sets))
    pulled = pulled_sum.reshape(NODES, width).astype(jnp.bfloat16)
    input_grad = jnp.dot(pulled, weight.T, preferred_element_type=jnp.float32).astype(jnp.bfloat16)
    weight_grad = jnp.dot(features.T, pulled, preferred_element_type=jnp.float32)
    return hidden.reshape(NODES, width), input_grad, weight_grad
```

```python
import functools

import jax
import jax.numpy as jnp
from jax import lax
from jax.experimental import pallas as pl
from jax.experimental.pallas import tpu as pltpu
from jax.sharding import PartitionSpec as P

MESH = pl.DeviceIdType.MESH
X, ZL, ZH, Y = 4, 8, 2, 4
T = 128


def dot(a, b):
    return jnp.dot(a, b, preferred_element_type=jnp.float32)


def kernel(
    table,
    feat,
    weight,
    up,
    adj_hbm,
    hidden,
    input_grad,
    weight_grad,
    adj,
    feats,
    sums,
    c1_out,
    c1_in,
    c2_out,
    c2_in,
    part,
    c3_out,
    c3_in,
    slopes,
    terms,
    gx_in,
    gz_out,
    gz_in,
    wg_out,
    h1_in,
    h2_buf,
    h3_buf,
    wg_all,
    adj_sem,
    az_s,
    az_r,
    ax_s,
    ax_r,
    c1_s,
    c1_r,
    c2_s,
    c2_r,
    c3_s,
    c3_r,
    e1_s,
    e1_r,
    e2_s,
    e2_r,
    e3_s,
    e3_r,
    gx_s,
    gx_r,
    gz_s,
    gz_r,
    h1_s,
    h1_r,
    h2_s,
    h2_r,
    h3_s,
    h3_r,
    h4_s,
    h4_r,
):
    BLK, REP = X * ZL, ZH * Y * 2
    SL = 2 * BLK
    f32, bf16 = jnp.float32, jnp.bfloat16
    b = lax.axis_index("blk")
    r = lax.axis_index("rep")
    x, z = b // ZL, b % ZL
    zh, y, core = r // (2 * Y), (r // 2) % Y, r % 2
    ozh = (zh + 1) % ZH
    b_up, b_dn = (b + 1) % BLK, (b + BLK - 1) % BLK

    def at_z(d):
        return (x * ZL + (z + d) % ZL, r)

    def at_x(d):
        return (((x + d) % X) * ZL + z, r)

    def rep_of(h, v, c):
        return (h * Y + v) * 2 + c

    def at_y(d):
        return (b, rep_of(zh, (y + d) % Y, core))

    sib = (b, rep_of(zh, y, 1 - core))
    r_oz = rep_of(ozh, y, core)

    def rc(src, dst, ss, rs, dev):
        return pltpu.make_async_remote_copy(
            src_ref=src, dst_ref=dst, send_sem=ss, recv_sem=rs, device_id=dev, device_id_type=MESH
        )

    load = pltpu.make_async_copy(adj_hbm, adj, adj_sem)
    load.start()

    bar = pltpu.get_barrier_semaphore()

    def greet(dev):
        pl.semaphore_signal(bar, inc=1, device_id=dev, device_id_type=MESH)

    for d in range(1, ZL):
        greet(at_z(d))
    for d in range(1, X):
        greet(at_x(d))
    for dev in ((b_up, r), (b_dn, r), (b_up, r_oz), (b_dn, r_oz)):
        greet(dev)
    for d in range(1, REP):
        greet((b, (r + d) % REP))
    pl.semaphore_wait(bar, (ZL - 1) + (X - 1) + 4 + (REP - 1))

    sends = []

    def go(copy):
        copy.start()
        sends.append(copy)
        return copy

    for d in range(1, ZL):
        go(rc(feat, feats.at[b], az_s.at[d], az_r.at[d], at_z(d)))
    for e in range(1, X):
        go(rc(feat, feats.at[b], ax_s.at[e, 0], ax_r.at[e, 0], at_x(e)))
    feats[b] = feat[...]
    sums[2 * SL] = jnp.zeros((T, T), f32)
    slopes[2 * REP] = jnp.zeros((T, T), bf16)
    for d in range(1, ZL):
        n = x * ZL + (z + ZL - d) % ZL
        rc(feat, feats.at[n], az_s.at[d], az_r.at[d], at_z(d)).wait_recv()
        for e in range(1, X):
            go(rc(feats.at[n], feats.at[n], ax_s.at[e, d], ax_r.at[e, d], at_x(e)))
    for d in range(0, ZL):
        for e in range(1, X):
            n = ((x + X - e) % X) * ZL + (z + ZL - d) % ZL
            rc(feat, feats.at[n], ax_s.at[e, d], ax_r.at[e, d], at_x(e)).wait_recv()
    load.wait()

    w = weight[...]

    def forward(n, carry):
        mixed = dot(feats[n], w).astype(bf16)
        for s in range(2):
            q = s * SL + 2 * n
            a = adj[pl.ds(q, 2)].reshape(2 * T, T)
            prod = dot(a, mixed)
            sums[q] = prod[:T] + sums[table[q]]
            sums[q + 1] = prod[T:] + sums[table[q + 1]]
        return carry

    lax.fori_loop(0, BLK, forward, 0)

    def routed(s, t):
        return sums[table[2 * SL + s * REP + t]]

    order = tuple(range(1, Y)) + (0,)
    for d in order:
        yy = (y + d) % Y
        for s in range(2):
            for h in range(ZH):
                c1_out[d, s * ZH + h] = routed(s, rep_of(h, yy, 1 - core)).astype(bf16)
        go(rc(c1_out.at[d], c1_in.at[d], c1_s.at[d], c1_r.at[d], sib))
    for d in order:
        yy = (y + d) % Y
        rc(c1_out.at[d], c1_in.at[d], c1_s.at[d], c1_r.at[d], sib).wait_recv()
        for s in range(2):
            for h in range(ZH):
                both = routed(s, rep_of(h, yy, core)) + c1_in[d, s * ZH + h].astype(f32)
                if d:
                    c2_out[d, s * ZH + h] = both.astype(bf16)
                else:
                    part[s * ZH + h] = both
        if d:
            go(rc(c2_out.at[d], c2_in.at[d], c2_s.at[d], c2_r.at[d], at_y(d)))
    for d in range(1, Y):
        rc(c2_out.at[d], c2_in.at[d], c2_s.at[d], c2_r.at[d], at_y(d)).wait_recv()
    for i in range(2 * ZH):
        total = part[i]
        for d in range(1, Y):
            total = total + c2_in[d, i].astype(f32)
        part[i] = total
    c3_to = ((b, r_oz), (b_dn, r_oz), (b_dn, r))
    for i, pick in enumerate((ozh, ZH + ozh, ZH + zh)):
        c3_out[i] = part[pick].astype(bf16)
        go(rc(c3_out.at[i], c3_in.at[i], c3_s.at[i], c3_r.at[i], c3_to[i]))
    summed = part[zh]
    for i in range(3):
        rc(c3_out.at[i], c3_in.at[i], c3_s.at[i], c3_r.at[i], c3_to[i]).wait_recv()
        summed = summed + c3_in[i].astype(f32)

    sig = jax.nn.sigmoid(summed)
    slope = up[...].astype(f32) * (sig * (1.0 + summed * (1.0 - sig)))

    def place(s, h, v, c):
        return ((c * Y + v) * 2 + s) * ZH + h

    mine, helps = place(0, zh, y, core), place(1, zh, y, core)
    slopes[mine] = slope.T.astype(bf16)
    own = slopes.at[mine]
    e1 = (
        (slopes.at[mine], (b, r_oz)),
        (slopes.at[helps], (b_up, r_oz)),
        (slopes.at[helps], (b_up, r)),
    )
    for i, (dst, dev) in enumerate(e1):
        go(rc(own, dst, e1_s.at[i], e1_r.at[i], dev))
    hidden[...] = (summed * sig).astype(bf16)
    for i, (dst, dev) in enumerate(e1):
        rc(own, dst, e1_s.at[i], e1_r.at[i], dev).wait_recv()

    def chunk(v, c):
        return slopes.at[pl.ds((c * Y + v) * 2 * ZH, 2 * ZH)]

    for d in range(1, Y):
        go(rc(chunk(y, core), chunk(y, core), e2_s.at[d], e2_r.at[d], at_y(d)))
    go(rc(chunk(y, core), chunk(y, core), e3_s.at[0], e3_r.at[0], sib))
    for d in range(1, Y):
        v = (y + Y - d) % Y
        rc(chunk(v, core), chunk(v, core), e2_s.at[d], e2_r.at[d], at_y(d)).wait_recv()
        go(rc(chunk(v, core), chunk(v, core), e3_s.at[d], e3_r.at[d], sib))
    for d in range(Y):
        v = (y + Y - d) % Y
        got = chunk(v, 1 - core)
        rc(got, got, e3_s.at[d], e3_r.at[d], sib).wait_recv()

    base = 2 * SL + 2 * REP

    def backward(n, total):
        out = None
        for s in range(2):
            q = s * SL + 2 * n
            lhs = jnp.concatenate(
                [slopes[table[base + q]], slopes[table[base + q + 1]]], axis=1
            )
            term = dot(lhs, adj[pl.ds(q, 2)].reshape(2 * T, T))
            out = term if out is None else out + term
        out = out.astype(bf16)
        terms[n] = out
        return total + dot(out, feats[n])

    total = jnp.zeros((T, T), f32)
    for e in tuple(range(1, X)) + (0,):
        first = ((x + e) % X) * ZL
        total = lax.fori_loop(0, ZL, lambda i, t: backward(first + i, t), total)
        if e:
            go(rc(terms.at[pl.ds(first, ZL)], gx_in.at[e], gx_s.at[e], gx_r.at[e], at_x(e)))

    wg_out[...] = total.reshape(REP, T // REP, T)

    def h1(d):
        q = (r + d) % REP
        return rc(wg_out.at[q], h1_in.at[d], h1_s.at[d], h1_r.at[d], (b, q))

    def loop(lo, hi, body):
        def step(i, c):
            body(i)
            return c

        lax.fori_loop(lo, hi, step, 0)

    loop(1, REP, lambda d: h1(d).start())

    for e in range(1, X):
        rc(gx_in.at[e], gx_in.at[e], gx_s.at[e], gx_r.at[e], at_x(e)).wait_recv()
    kept = None
    for d in tuple(range(1, ZL)) + (0,):
        v = (z + d) % ZL
        s = terms[x * ZL + v].astype(f32)
        for e in range(1, X):
            s = s + gx_in[e, v].astype(f32)
        if d:
            gz_out[d] = s.astype(bf16)
            go(rc(gz_out.at[d], gz_in.at[d], gz_s.at[d], gz_r.at[d], at_z(d)))
        else:
            kept = s

    loop(1, REP, lambda d: h1(d).wait_recv())
    unit = wg_out[r]
    for d in range(1, REP):
        unit = unit + h1_in[d]
    h2_buf[x] = unit
    for e in range(1, X):
        go(rc(h2_buf.at[x], h2_buf.at[x], h2_s.at[e], h2_r.at[e], at_x(e)))
    for e in range(1, X):
        v = (x + X - e) % X
        rc(h2_buf.at[v], h2_buf.at[v], h2_s.at[e], h2_r.at[e], at_x(e)).wait_recv()
    unit = h2_buf[0]
    for e in range(1, X):
        unit = unit + h2_buf[e]
    h3_buf[z] = unit
    for d in range(1, ZL):
        go(rc(h3_buf.at[z], h3_buf.at[z], h3_s.at[d], h3_r.at[d], at_z(d)))

    for d in range(1, ZL):
        rc(gz_out.at[d], gz_in.at[d], gz_s.at[d], gz_r.at[d], at_z(d)).wait_recv()
        kept = kept + gz_in[d].astype(f32)

    for d in range(1, ZL):
        v = (z + ZL - d) % ZL
        rc(h3_buf.at[v], h3_buf.at[v], h3_s.at[d], h3_r.at[d], at_z(d)).wait_recv()
    unit = h3_buf[0]
    for d in range(1, ZL):
        unit = unit + h3_buf[d]
    wg_all[r] = unit

    def h4(d, to):
        q = (r + REP - d) % REP
        slot = wg_all.at[r] if to else wg_all.at[q]
        return rc(slot, slot, h4_s.at[d], h4_r.at[d], (b, (r + d) % REP))

    loop(1, REP, lambda d: h4(d, True).start())

    pulled = kept.T.astype(bf16)
    input_grad[...] = lax.dot_general(
        pulled, w, (((1,), (1,)), ((), ())), preferred_element_type=f32
    ).astype(bf16)

    loop(1, REP, lambda d: h4(d, False).wait_recv())
    weight_grad[...] = wg_all[...].reshape(T, T).T

    for copy in sends:
        copy.wait_send()
    loop(1, REP, lambda d: h1(d).wait_send())
    loop(1, REP, lambda d: h4(d, True).wait_send())


def tables(row_tiles, live_counts, blocks, reps):
    slots = 2 * blocks
    row = row_tiles.reshape(2, slots)
    count = jnp.repeat(live_counts.reshape(2, blocks), 2, axis=1)
    q = jnp.arange(slots, dtype=jnp.int32)
    alive = (q % 2)[None] < count
    key = jnp.where(alive, row, reps)
    want = jnp.concatenate(
        [key, jnp.broadcast_to(jnp.arange(reps, dtype=jnp.int32), (2, reps))], axis=1
    )
    limit = jnp.concatenate([q, jnp.full((reps,), slots, jnp.int32)])
    hit = (
        (key[:, None, :] == want[:, :, None])
        & alive[:, None, :]
        & (q[None, None, :] < limit[None, :, None])
    )
    at = q[None] + slots * jnp.arange(2, dtype=jnp.int32)[:, None]
    found = jnp.max(jnp.where(hit, at[:, None, :], -1), axis=2)
    found = jnp.where(found < 0, 2 * slots, found)
    h, v, c = row // (2 * Y), (row // 2) % Y, row % 2
    s = jnp.arange(2, dtype=jnp.int32)[:, None]
    pos = jnp.where(alive, ((c * Y + v) * 2 + s) * ZH + h, 2 * reps)
    return jnp.concatenate(
        [found[:, :slots].reshape(-1), found[:, slots:].reshape(-1), pos.reshape(-1)]
    )


def local(features, weight, adjacency, row_tiles, live_counts, upstream):
    BLK, REP = X * ZL, ZH * Y * 2
    f32, bf16 = jnp.float32, jnp.bfloat16
    table = tables(row_tiles, live_counts, BLK, REP)
    adj = adjacency.reshape(4 * BLK, T, T)
    vmem = pl.BlockSpec(memory_space=pltpu.VMEM)

    def buf(*dims, dtype=bf16):
        return pltpu.VMEM(dims + (T,), dtype)

    U = T // REP
    dma = pltpu.SemaphoreType.DMA
    scratch = [
        buf(4 * BLK, T),
        buf(BLK, T),
        buf(4 * BLK + 1, T, dtype=f32),
        buf(Y, 2 * ZH, T),
        buf(Y, 2 * ZH, T),
        buf(Y, 2 * ZH, T),
        buf(Y, 2 * ZH, T),
        buf(2 * ZH, T, dtype=f32),
        buf(3, T),
        buf(3, T),
        buf(2 * REP + 1, T),
        buf(BLK, T),
        buf(X, ZL, T),
        buf(ZL, T),
        buf(ZL, T),
        buf(REP, U, dtype=f32),
        buf(REP, U, dtype=f32),
        buf(X, U, dtype=f32),
        buf(ZL, U, dtype=f32),
        buf(REP, U, dtype=f32),
        dma,
        dma((ZL,)),
        dma((ZL,)),
        dma((X, ZL)),
        dma((X, ZL)),
        dma((Y,)),
        dma((Y,)),
        dma((Y,)),
        dma((Y,)),
        dma((3,)),
        dma((3,)),
        dma((3,)),
        dma((3,)),
        dma((Y,)),
        dma((Y,)),
        dma((Y,)),
        dma((Y,)),
        dma((X,)),
        dma((X,)),
        dma((ZL,)),
        dma((ZL,)),
        dma((REP,)),
        dma((REP,)),
        dma((X,)),
        dma((X,)),
        dma((ZL,)),
        dma((ZL,)),
        dma((REP,)),
        dma((REP,)),
    ]
    return pl.pallas_call(
        kernel,
        name="graph_layer",
        out_shape=(
            jax.ShapeDtypeStruct((T, T), bf16),
            jax.ShapeDtypeStruct((T, T), bf16),
            jax.ShapeDtypeStruct((T, T), f32),
        ),
        in_specs=[
            pl.BlockSpec(memory_space=pltpu.SMEM),
            vmem,
            vmem,
            vmem,
            pl.BlockSpec(memory_space=pl.ANY),
        ],
        out_specs=(vmem, vmem, vmem),
        scratch_shapes=scratch,
        compiler_params=pltpu.CompilerParams(
            collective_id=0, has_side_effects=True, vmem_limit_bytes=48 * 1024 * 1024
        ),
    )(table, features, weight, upstream, adj)


def solution(mesh):
    assert mesh.shape["blk"] == X * ZL and mesh.shape["rep"] == ZH * Y * 2
    in_specs = (
        P(("blk", "rep"), None),
        P(),
        P("blk", "rep", None, None, None, None, None),
        P("blk", "rep", None, None, None),
        P("blk", "rep", None, None),
        P(("blk", "rep"), None),
    )
    out_specs = (P(("blk", "rep"), None), P(("blk", "rep"), None), P())
    return jax.shard_map(local, mesh=mesh, in_specs=in_specs, out_specs=out_specs, check_vma=False)
```

```python
import functools

import jax
import jax.numpy as jnp
from jax import lax
from jax.experimental import pallas as pl
from jax.experimental.pallas import tpu as pltpu
from jax.sharding import PartitionSpec as P

MESH = pl.DeviceIdType.MESH
X, ZL, ZH, Y = 4, 8, 2, 4
ZQ = ZL // 2
T = 128


def dot(a, b):
    return jnp.dot(a, b, preferred_element_type=jnp.float32)


def kernel(
    table,
    feat,
    weight,
    up,
    adj_hbm,
    hidden,
    input_grad,
    weight_grad,
    adj,
    feats,
    sums,
    c1_out,
    c1_in,
    c2_out,
    c2_in,
    part,
    c3_out,
    c3_in,
    slopes,
    terms,
    gx_in,
    gz_out,
    gz_in,
    gz2_out,
    gz2_in,
    wg_out,
    h0_in,
    halves,
    h1_in,
    h2_buf,
    h3_buf,
    wg_all,
    adj_sem,
    az_s,
    az_r,
    ax_s,
    ax_r,
    c1_s,
    c1_r,
    c2_s,
    c2_r,
    c3_s,
    c3_r,
    e1_s,
    e1_r,
    e2_s,
    e2_r,
    e3_s,
    e3_r,
    gx_s,
    gx_r,
    gz_s,
    gz_r,
    gz2_s,
    gz2_r,
    h0_s,
    h0_r,
    h1_s,
    h1_r,
    h2_s,
    h2_r,
    h3_s,
    h3_r,
    h4_s,
    h4_r,
    h5_s,
    h5_r,
):
    BLK, REP = X * ZL, ZH * Y * 2
    SL = 2 * BLK
    f32, bf16 = jnp.float32, jnp.bfloat16
    b = lax.axis_index("blk")
    r = lax.axis_index("rep")
    x, z = b // ZL, b % ZL
    zh, y, core = r // (2 * Y), (r // 2) % Y, r % 2
    ozh = (zh + 1) % ZH
    b_up, b_dn = (b + 1) % BLK, (b + BLK - 1) % BLK

    def at_z(d):
        return (x * ZL + (z + d) % ZL, r)

    def at_x(d):
        return (((x + d) % X) * ZL + z, r)

    def rep_of(h, v, c):
        return (h * Y + v) * 2 + c

    def at_y(d):
        return (b, rep_of(zh, (y + d) % Y, core))

    sib = (b, rep_of(zh, y, 1 - core))
    r_oz = rep_of(ozh, y, core)

    def rc(src, dst, ss, rs, dev):
        return pltpu.make_async_remote_copy(
            src_ref=src, dst_ref=dst, send_sem=ss, recv_sem=rs, device_id=dev, device_id_type=MESH
        )

    load = pltpu.make_async_copy(adj_hbm, adj, adj_sem)
    load.start()

    bar = pltpu.get_barrier_semaphore()

    def greet(dev):
        pl.semaphore_signal(bar, inc=1, device_id=dev, device_id_type=MESH)

    for i in range(1, ZH * ZL):
        greet((x * ZL + (z + i % ZL) % ZL, rep_of((zh + i // ZL) % ZH, y, core)))
    for d in range(1, X):
        greet(at_x(d))
    for d in range(1, Y):
        greet(at_y(d))
    for dev in (sib, (b_up, r), (b_dn, r), (b_up, r_oz), (b_dn, r_oz)):
        greet(dev)
    pl.semaphore_wait(bar, (ZH * ZL - 1) + (X - 1) + (Y - 1) + 5)

    sends = []

    def go(copy):
        copy.start()
        sends.append(copy)
        return copy

    for d in range(1, ZL):
        go(rc(feat, feats.at[b], az_s.at[d], az_r.at[d], at_z(d)))
    for e in range(1, X):
        go(rc(feat, feats.at[b], ax_s.at[e, 0], ax_r.at[e, 0], at_x(e)))
    feats[b] = feat[...]
    sums[2 * SL] = jnp.zeros((T, T), f32)
    slopes[2 * REP] = jnp.zeros((T, T), bf16)
    for d in range(1, ZL):
        n = x * ZL + (z + ZL - d) % ZL
        rc(feat, feats.at[n], az_s.at[d], az_r.at[d], at_z(d)).wait_recv()
        for e in range(1, X):
            go(rc(feats.at[n], feats.at[n], ax_s.at[e, d], ax_r.at[e, d], at_x(e)))
    for d in range(0, ZL):
        for e in range(1, X):
            n = ((x + X - e) % X) * ZL + (z + ZL - d) % ZL
            rc(feat, feats.at[n], ax_s.at[e, d], ax_r.at[e, d], at_x(e)).wait_recv()
    load.wait()

    w = weight[...]

    def forward(n, carry):
        mixed = dot(feats[n], w).astype(bf16)
        for s in range(2):
            q = s * SL + 2 * n
            a = adj[pl.ds(q, 2)].reshape(2 * T, T)
            prod = dot(a, mixed)
            sums[q] = prod[:T] + sums[table[q]]
            sums[q + 1] = prod[T:] + sums[table[q + 1]]
        return carry

    lax.fori_loop(0, BLK, forward, 0)

    def routed(s, t):
        return sums[table[2 * SL + s * REP + t]]

    order = tuple(range(1, Y)) + (0,)
    for d in order:
        yy = (y + d) % Y
        for s in range(2):
            for h in range(ZH):
                c1_out[d, s * ZH + h] = routed(s, rep_of(h, yy, 1 - core)).astype(bf16)
        go(rc(c1_out.at[d], c1_in.at[d], c1_s.at[d], c1_r.at[d], sib))
    for d in order:
        yy = (y + d) % Y
        rc(c1_out.at[d], c1_in.at[d], c1_s.at[d], c1_r.at[d], sib).wait_recv()
        for s in range(2):
            for h in range(ZH):
                both = routed(s, rep_of(h, yy, core)) + c1_in[d, s * ZH + h].astype(f32)
                if d:
                    c2_out[d, s * ZH + h] = both.astype(bf16)
                else:
                    part[s * ZH + h] = both
        if d:
            go(rc(c2_out.at[d], c2_in.at[d], c2_s.at[d], c2_r.at[d], at_y(d)))
    for d in range(1, Y):
        rc(c2_out.at[d], c2_in.at[d], c2_s.at[d], c2_r.at[d], at_y(d)).wait_recv()
    for i in range(2 * ZH):
        total = part[i]
        for d in range(1, Y):
            total = total + c2_in[d, i].astype(f32)
        part[i] = total
    c3_to = ((b, r_oz), (b_dn, r_oz), (b_dn, r))
    for i, pick in enumerate((ozh, ZH + ozh, ZH + zh)):
        c3_out[i] = part[pick].astype(bf16)
        go(rc(c3_out.at[i], c3_in.at[i], c3_s.at[i], c3_r.at[i], c3_to[i]))
    summed = part[zh]
    for i in range(3):
        rc(c3_out.at[i], c3_in.at[i], c3_s.at[i], c3_r.at[i], c3_to[i]).wait_recv()
        summed = summed + c3_in[i].astype(f32)

    sig = jax.nn.sigmoid(summed)
    slope = up[...].astype(f32) * (sig * (1.0 + summed * (1.0 - sig)))

    def place(s, h, v, c):
        return ((c * Y + v) * 2 + s) * ZH + h

    kinds = ((0, zh), (1, zh), (0, ozh), (1, ozh))

    def tile(j, v, c):
        return slopes.at[place(*kinds[j], v, c)]

    slopes[place(0, zh, y, core)] = slope.T.astype(bf16)
    own, helps = tile(0, y, core), tile(1, y, core)
    e1 = ((own, (b, r_oz)), (helps, (b_up, r_oz)), (helps, (b_up, r)))

    def e1_copy(i):
        dst, dev = e1[i]
        return rc(own, dst, e1_s.at[i], e1_r.at[i], dev)

    def e2_copy(j, d, v):
        return rc(tile(j, v, core), tile(j, v, core), e2_s.at[j, d], e2_r.at[j, d], at_y(d))

    def e3_copy(j, d, c):
        got = tile(j, (y + Y - d) % Y, c)
        return rc(got, got, e3_s.at[j, d], e3_r.at[j, d], sib)

    def spread(j):
        for d in range(1, Y):
            go(e2_copy(j, d, y))
        go(e3_copy(j, 0, core))

    def pass_on(j):
        for d in range(1, Y):
            e2_copy(j, d, (y + Y - d) % Y).wait_recv()
            go(e3_copy(j, d, core))

    for i in range(3):
        go(e1_copy(i))
    spread(0)
    hidden[...] = (summed * sig).astype(bf16)
    e1_copy(2).wait_recv()
    spread(1)
    pass_on(0)
    e1_copy(0).wait_recv()
    spread(2)
    e1_copy(1).wait_recv()
    spread(3)
    for j in range(1, 4):
        pass_on(j)
    for j in range(4):
        for d in range(Y):
            e3_copy(j, d, 1 - core).wait_recv()

    base = 2 * SL + 2 * REP
    half, zq = z // ZQ, z % ZQ
    ohalf = 1 - half

    def backward(n):
        out = None
        for s in range(2):
            q = s * SL + 2 * n
            lhs = jnp.concatenate(
                [slopes[table[base + q]], slopes[table[base + q + 1]]], axis=1
            )
            term = dot(lhs, adj[pl.ds(q, 2)].reshape(2 * T, T))
            out = term if out is None else out + term
        out = out.astype(bf16)
        terms[n] = out
        return dot(out, feats[n])

    def gx_copy(k, e):
        first = ((x + e) % X) * ZL + (ohalf, half)[k] * ZQ
        return rc(terms.at[pl.ds(first, ZQ)], gx_in.at[k, e], gx_s.at[k, e], gx_r.at[k, e], at_x(e))

    total = jnp.zeros((T, T), f32)
    for k in range(2):
        for e in tuple(range(1, X)) + (0,):
            first = ((x + e) % X) * ZL + (ohalf, half)[k] * ZQ
            for i in range(ZQ):
                total = total + backward(first + i)
            if e:
                go(gx_copy(k, e))

    U = T // (2 * Y)
    wg_out[...] = total.reshape(2 * Y, U, T)

    def h0_copy():
        return rc(wg_out.at[pl.ds((1 - core) * Y, Y)], h0_in, h0_s, h0_r, sib)

    go(h0_copy())

    def gx_sum(k, v):
        t = terms[x * ZL + (ohalf, half)[k] * ZQ + v].astype(f32)
        for e in range(1, X):
            t = t + gx_in[k, e, v].astype(f32)
        return t

    def gz_copy(k, m):
        v = (zq + m) % ZQ
        return rc(
            gz_out.at[k, m],
            gz_in.at[k, m],
            gz_s.at[k, m],
            gz_r.at[k, m],
            (x * ZL + half * ZQ + v, r),
        )

    def gx_wait(k):
        for e in range(1, X):
            gx_copy(k, e).wait_recv()
        for m in range(1, ZQ):
            gz_out[k, m] = gx_sum(k, (zq + m) % ZQ).astype(bf16)
            go(gz_copy(k, m))
        return gx_sum(k, zq)

    def h1_copy(d):
        return rc(halves.at[(y + d) % Y], h1_in.at[d], h1_s.at[d], h1_r.at[d], at_y(d))

    h0_copy().wait_recv()
    halves[...] = wg_out[pl.ds(core * Y, Y)] + h0_in[...]
    for d in range(1, Y):
        go(h1_copy(d))

    crossing = gx_wait(0)

    zz = zh * ZL + z

    def h2_copy(i, to):
        h, d = (zh + i // ZL) % ZH, i % ZL
        v = (z + (d if to else ZL - d)) % ZL
        slot = h2_buf.at[zz] if to else h2_buf.at[h * ZL + v]
        dev = (x * ZL + v, rep_of(h, y, core))
        return rc(slot, slot, h2_s.at[i], h2_r.at[i], dev)

    unit = halves[y]
    for d in range(1, Y):
        h1_copy(d).wait_recv()
        unit = unit + h1_in[d]
    h2_buf[zz] = unit.astype(bf16)
    for i in range(1, ZH * ZL):
        go(h2_copy(i, True))

    kept = gx_wait(1)

    def gz2_copy():
        return rc(gz2_out, gz2_in, gz2_s, gz2_r, (x * ZL + ohalf * ZQ + zq, r))

    for m in range(1, ZQ):
        gz_copy(0, m).wait_recv()
        crossing = crossing + gz_in[0, m].astype(f32)
    gz2_out[...] = crossing.astype(bf16)
    go(gz2_copy())
    for m in range(1, ZQ):
        gz_copy(1, m).wait_recv()
        kept = kept + gz_in[1, m].astype(f32)

    def h3_copy(e, v):
        return rc(h3_buf.at[v], h3_buf.at[v], h3_s.at[e], h3_r.at[e], at_x(e))

    for i in range(1, ZH * ZL):
        h2_copy(i, False).wait_recv()
    unit = h2_buf[0].astype(f32)
    for i in range(1, ZH * ZL):
        unit = unit + h2_buf[i].astype(f32)
    h3_buf[x] = unit
    for e in range(1, X):
        go(h3_copy(e, x))

    gz2_copy().wait_recv()
    pulled = (kept + gz2_in[...].astype(f32)).T.astype(bf16)
    input_grad[...] = lax.dot_general(
        pulled, w, (((1,), (1,)), ((), ())), preferred_element_type=f32
    ).astype(bf16)

    def h4_copy(d, v):
        slot = wg_all.at[core * Y + v]
        return rc(slot, slot, h4_s.at[d], h4_r.at[d], at_y(d))

    def h5_copy(d, c):
        slot = wg_all.at[c * Y + (y + Y - d) % Y]
        return rc(slot, slot, h5_s.at[d], h5_r.at[d], sib)

    for e in range(1, X):
        h3_copy(e, (x + X - e) % X).wait_recv()
    unit = h3_buf[0]
    for e in range(1, X):
        unit = unit + h3_buf[e]
    wg_all[core * Y + y] = unit
    for d in range(1, Y):
        go(h4_copy(d, y))
    go(h5_copy(0, core))
    for d in range(1, Y):
        h4_copy(d, (y + Y - d) % Y).wait_recv()
        go(h5_copy(d, core))
    for d in range(Y):
        h5_copy(d, 1 - core).wait_recv()
    weight_grad[...] = wg_all[...].reshape(T, T).T

    for copy in sends:
        copy.wait_send()


def tables(row_tiles, live_counts, blocks, reps):
    slots = 2 * blocks
    row = row_tiles.reshape(2, slots)
    count = jnp.repeat(live_counts.reshape(2, blocks), 2, axis=1)
    q = jnp.arange(slots, dtype=jnp.int32)
    alive = (q % 2)[None] < count
    key = jnp.where(alive, row, reps)
    want = jnp.concatenate(
        [key, jnp.broadcast_to(jnp.arange(reps, dtype=jnp.int32), (2, reps))], axis=1
    )
    limit = jnp.concatenate([q, jnp.full((reps,), slots, jnp.int32)])
    hit = (
        (key[:, None, :] == want[:, :, None])
        & alive[:, None, :]
        & (q[None, None, :] < limit[None, :, None])
    )
    at = q[None] + slots * jnp.arange(2, dtype=jnp.int32)[:, None]
    found = jnp.max(jnp.where(hit, at[:, None, :], -1), axis=2)
    found = jnp.where(found < 0, 2 * slots, found)
    h, v, c = row // (2 * Y), (row // 2) % Y, row % 2
    s = jnp.arange(2, dtype=jnp.int32)[:, None]
    pos = jnp.where(alive, ((c * Y + v) * 2 + s) * ZH + h, 2 * reps)
    return jnp.concatenate(
        [found[:, :slots].reshape(-1), found[:, slots:].reshape(-1), pos.reshape(-1)]
    )


def local(features, weight, adjacency, row_tiles, live_counts, upstream):
    BLK, REP = X * ZL, ZH * Y * 2
    f32, bf16 = jnp.float32, jnp.bfloat16
    table = tables(row_tiles, live_counts, BLK, REP)
    adj = adjacency.reshape(4 * BLK, T, T)
    vmem = pl.BlockSpec(memory_space=pltpu.VMEM)

    def buf(*dims, dtype=bf16):
        return pltpu.VMEM(dims + (T,), dtype)

    U = T // (2 * Y)
    dma = pltpu.SemaphoreType.DMA
    scratch = [
        buf(4 * BLK, T),
        buf(BLK, T),
        buf(4 * BLK + 1, T, dtype=f32),
        buf(Y, 2 * ZH, T),
        buf(Y, 2 * ZH, T),
        buf(Y, 2 * ZH, T),
        buf(Y, 2 * ZH, T),
        buf(2 * ZH, T, dtype=f32),
        buf(3, T),
        buf(3, T),
        buf(2 * REP + 1, T),
        buf(BLK, T),
        buf(2, X, ZQ, T),
        buf(2, ZQ, T),
        buf(2, ZQ, T),
        buf(T),
        buf(T),
        buf(2 * Y, U, dtype=f32),
        buf(Y, U, dtype=f32),
        buf(Y, U, dtype=f32),
        buf(Y, U, dtype=f32),
        buf(ZH * ZL, U),
        buf(X, U, dtype=f32),
        buf(2 * Y, U, dtype=f32),
        dma,
        dma((ZL,)),
        dma((ZL,)),
        dma((X, ZL)),
        dma((X, ZL)),
        dma((Y,)),
        dma((Y,)),
        dma((Y,)),
        dma((Y,)),
        dma((3,)),
        dma((3,)),
        dma((3,)),
        dma((3,)),
        dma((4, Y)),
        dma((4, Y)),
        dma((4, Y)),
        dma((4, Y)),
        dma((2, X)),
        dma((2, X)),
        dma((2, ZQ)),
        dma((2, ZQ)),
        dma,
        dma,
        dma,
        dma,
        dma((Y,)),
        dma((Y,)),
        dma((ZH * ZL,)),
        dma((ZH * ZL,)),
        dma((X,)),
        dma((X,)),
        dma((Y,)),
        dma((Y,)),
        dma((Y,)),
        dma((Y,)),
    ]
    return pl.pallas_call(
        kernel,
        name="graph_layer",
        out_shape=(
            jax.ShapeDtypeStruct((T, T), bf16),
            jax.ShapeDtypeStruct((T, T), bf16),
            jax.ShapeDtypeStruct((T, T), f32),
        ),
        in_specs=[
            pl.BlockSpec(memory_space=pltpu.SMEM),
            vmem,
            vmem,
            vmem,
            pl.BlockSpec(memory_space=pl.ANY),
        ],
        out_specs=(vmem, vmem, vmem),
        scratch_shapes=scratch,
        compiler_params=pltpu.CompilerParams(
            collective_id=0, has_side_effects=True, vmem_limit_bytes=48 * 1024 * 1024
        ),
    )(table, features, weight, upstream, adj)


def solution(mesh):
    assert mesh.shape["blk"] == X * ZL and mesh.shape["rep"] == ZH * Y * 2
    in_specs = (
        P(("blk", "rep"), None),
        P(),
        P("blk", "rep", None, None, None, None, None),
        P("blk", "rep", None, None, None),
        P("blk", "rep", None, None),
        P(("blk", "rep"), None),
    )
    out_specs = (P(("blk", "rep"), None), P(("blk", "rep"), None), P())
    return jax.shard_map(local, mesh=mesh, in_specs=in_specs, out_specs=out_specs, check_vma=False)
```

```python
import functools

import jax
import jax.numpy as jnp
from jax import lax
from jax.experimental import pallas as pl
from jax.experimental.pallas import tpu as pltpu
from jax.sharding import PartitionSpec as P

MESH = pl.DeviceIdType.MESH
X, ZL, ZH, Y = 4, 8, 2, 4
ZQ = ZL // 2
T = 128


def dot(a, b):
    return jnp.dot(a, b, preferred_element_type=jnp.float32)


def kernel(
    feat_hbm,
    weight_hbm,
    up_hbm,
    adj_hbm,
    rows_hbm,
    live_hbm,
    hidden,
    input_grad,
    weight_grad,
    adj,
    up,
    weight,
    rows_v,
    live_v,
    tab_v,
    table,
    feats,
    sums,
    c1_out,
    c1_in,
    c2_out,
    c2_in,
    part,
    c3_out,
    c3_in,
    slopes,
    terms,
    gx_in,
    gz_out,
    gz_in,
    gz2_out,
    gz2_in,
    wg_out,
    h0_in,
    halves,
    h1_in,
    h2_buf,
    h3_buf,
    wg_all,
    in_sem,
    az_s,
    az_r,
    ax_s,
    ax_r,
    c1_s,
    c1_r,
    c2_s,
    c2_r,
    c3_s,
    c3_r,
    e1_s,
    e1_r,
    e2_s,
    e2_r,
    e3_s,
    e3_r,
    gx_s,
    gx_r,
    gz_s,
    gz_r,
    gz2_s,
    gz2_r,
    h0_s,
    h0_r,
    h1_s,
    h1_r,
    h2_s,
    h2_r,
    h3_s,
    h3_r,
    h4_s,
    h4_r,
    h5_s,
    h5_r,
):
    BLK, REP = X * ZL, ZH * Y * 2
    SL = 2 * BLK
    f32, bf16 = jnp.float32, jnp.bfloat16
    b = lax.axis_index("blk")
    r = lax.axis_index("rep")
    x, z = b // ZL, b % ZL
    zh, y, core = r // (2 * Y), (r // 2) % Y, r % 2
    ozh = (zh + 1) % ZH
    b_up, b_dn = (b + 1) % BLK, (b + BLK - 1) % BLK

    def at_z(d):
        return (x * ZL + (z + d) % ZL, r)

    def at_x(d):
        return (((x + d) % X) * ZL + z, r)

    def rep_of(h, v, c):
        return (h * Y + v) * 2 + c

    def at_y(d):
        return (b, rep_of(zh, (y + d) % Y, core))

    sib = (b, rep_of(zh, y, 1 - core))
    r_oz = rep_of(ozh, y, core)

    def rc(src, dst, ss, rs, dev):
        return pltpu.make_async_remote_copy(
            src_ref=src, dst_ref=dst, send_sem=ss, recv_sem=rs, device_id=dev, device_id_type=MESH
        )

    in_copies = [
        pltpu.make_async_copy(src, dst, in_sem.at[i])
        for i, (src, dst) in enumerate(
            (
                (feat_hbm, feats.at[b]),
                (rows_hbm, rows_v),
                (live_hbm, live_v),
                (weight_hbm, weight),
                (adj_hbm, adj),
                (up_hbm, up),
            )
        )
    ]
    for copy in in_copies:
        copy.start()

    bar = pltpu.get_barrier_semaphore()

    def greet(dev):
        pl.semaphore_signal(bar, inc=1, device_id=dev, device_id_type=MESH)

    for i in range(1, ZH * ZL):
        greet((x * ZL + (z + i % ZL) % ZL, rep_of((zh + i // ZL) % ZH, y, core)))
    for d in range(1, X):
        greet(at_x(d))
    for d in range(1, Y):
        greet(at_y(d))
    for dev in (sib, (b_up, r), (b_dn, r), (b_up, r_oz), (b_dn, r_oz)):
        greet(dev)

    half, zq = z // ZQ, z % ZQ
    ohalf = 1 - half

    in_copies[1].wait()
    in_copies[2].wait()
    i_s = lax.broadcasted_iota(jnp.int32, (BLK, BLK), 0)
    i_l = lax.broadcasted_iota(jnp.int32, (BLK, BLK), 1)

    def rank(n):
        far = ((n // ZQ) % 2) ^ half
        return (far * ZQ + ((zq - n % ZQ) & (ZQ - 1))) * X + ((x - n // ZL) & (X - 1))

    rank_s, rank_l = rank(i_s), rank(i_l)

    def to_rows(lanes):
        return jnp.sum(jnp.where(i_s == i_l, lanes, 0), axis=1, keepdims=True)

    t_l = lax.broadcasted_iota(jnp.int32, (BLK, REP), 1)
    for s in range(2):
        row_s = [to_rows(rows_v[s, k : k + 1, :]) for k in range(2)]
        live_l = live_v[s : s + 1, :]
        live_s = to_rows(live_l)
        code = [(2 * rank_s + k) * 1024 + s * SL + 2 * i_s + k for k in range(2)]

        def best(hits):
            found = jnp.max(jnp.maximum(hits[0], hits[1]), axis=0, keepdims=True)
            return jnp.where(found < 0, 2 * SL, found & 1023)

        for k in range(2):
            row_l = rows_v[s, k : k + 1, :]
            hits = [
                jnp.where(
                    (row_s[o] == row_l) & (live_s > o) & (2 * rank_s + o < 2 * rank_l + k),
                    code[o],
                    -1,
                )
                for o in range(2)
            ]
            tab_v[2 * s + k : 2 * s + k + 1, :BLK] = best(hits)
            spot = ((((row_l & 1) * Y + ((row_l // 2) & (Y - 1))) * 2 + s) * ZH) + row_l // (2 * Y)
            tab_v[6 + 2 * s + k : 7 + 2 * s + k, :BLK] = jnp.where(live_l > k, spot, 2 * REP)
        hits = [
            jnp.where((row_s[o] == t_l) & (live_s > o), code[o][:, :1], -1) for o in range(2)
        ]
        tab_v[4 + s : 5 + s, :REP] = best(hits)
    to_scalars = pltpu.make_async_copy(tab_v, table, in_sem.at[6])
    to_scalars.start()
    sums[2 * SL] = jnp.zeros((T, T), f32)
    slopes[2 * REP] = jnp.zeros((T, T), bf16)
    in_copies[0].wait()
    in_copies[3].wait()

    sends = []

    def go(copy):
        copy.start()
        sends.append(copy)
        return copy

    pl.semaphore_wait(bar, (ZH * ZL - 1) + (X - 1) + (Y - 1) + 5)

    def zsrc(g):
        return (half, ohalf)[g // ZQ] * ZQ + (zq + ZQ - g % ZQ) % ZQ

    def mate(m):
        return (x * ZL + half * ZQ + (zq + m) % ZQ, r)

    partner = (x * ZL + ohalf * ZQ + zq, r)

    def az_copy(g, v, dev):
        slot = feats.at[x * ZL + v]
        return rc(slot, slot, az_s.at[g], az_r.at[g], dev)

    def ax_copy(g, e, v):
        slot = feats.at[v * ZL + zsrc(g)]
        return rc(slot, slot, ax_s.at[e, g], ax_r.at[e, g], at_x(e))

    def along_x(g):
        for e in range(1, X):
            go(ax_copy(g, e, x))

    go(az_copy(ZQ, z, partner))
    for m in range(1, ZQ):
        go(az_copy(m, z, mate(m)))
    along_x(0)
    for m in range(1, ZQ):
        az_copy(m, zsrc(m), mate(m)).wait_recv()
        along_x(m)
    az_copy(ZQ, zsrc(ZQ), partner).wait_recv()
    for m in range(1, ZQ):
        go(az_copy(ZQ + m, zsrc(ZQ), mate(m)))
    along_x(ZQ)
    in_copies[4].wait()
    to_scalars.wait()

    w = weight[...]

    def forward(g):
        for e in range(X):
            v = (x + X - e) % X
            if e:
                ax_copy(g, e, v).wait_recv()
            n = v * ZL + zsrc(g)
            mixed = dot(feats[n], w).astype(bf16)
            for s in range(2):
                q = s * SL + 2 * n
                prod = dot(adj[pl.ds(q, 2)].reshape(2 * T, T), mixed)
                sums[q] = prod[:T] + sums[table[2 * s, n]]
                sums[q + 1] = prod[T:] + sums[table[2 * s + 1, n]]

    early = ZQ - 1
    for g in range(early):
        forward(g)
    for m in range(1, ZQ):
        az_copy(ZQ + m, zsrc(ZQ + m), mate(m)).wait_recv()
        along_x(ZQ + m)
    for g in range(early, ZL):
        forward(g)

    def routed(s, t):
        return sums[table[4 + s, t]]

    order = tuple(range(1, Y)) + (0,)
    sides = (ozh, zh)

    def c1_copy(k, d):
        return rc(c1_out.at[k, d], c1_in.at[k, d], c1_s.at[k, d], c1_r.at[k, d], sib)

    def c2_copy(k, d):
        return rc(c2_out.at[k, d], c2_in.at[k, d], c2_s.at[k, d], c2_r.at[k, d], at_y(d))

    for k in range(2):
        for d in order:
            for s in range(2):
                c1_out[k, d, s] = routed(s, rep_of(sides[k], (y + d) % Y, 1 - core)).astype(bf16)
            go(c1_copy(k, d))
    for k in range(2):
        for d in order:
            c1_copy(k, d).wait_recv()
            for s in range(2):
                both = routed(s, rep_of(sides[k], (y + d) % Y, core)) + c1_in[k, d, s].astype(f32)
                if d:
                    c2_out[k, d, s] = both.astype(bf16)
                else:
                    part[k, s] = both
            if d:
                go(c2_copy(k, d))

    first, last = (ZL - z) // ZL, (z + 1) // ZL

    def c3_copy(i):
        dev = (
            (b, r_oz),
            (b_dn, r),
            (b_dn, rep_of((zh + first) % ZH, y, core)),
        )[i]
        return rc(c3_out.at[i], c3_in.at[i], c3_s.at[i], c3_r.at[i], dev)

    def reduced(k, s):
        t = part[k, s]
        for d in range(1, Y):
            t = t + c2_in[k, d, s].astype(f32)
        return t

    for k in range(2):
        for d in range(1, Y):
            c2_copy(k, d).wait_recv()
        c3_out[2 - k] = reduced(k, 1).astype(bf16)
        go(c3_copy(2 - k))
    c3_copy(2).wait_recv()
    near = c3_in[2].astype(f32)
    c3_out[0] = (reduced(0, 0) + jnp.where(last == 0, near, 0.0)).astype(bf16)
    go(c3_copy(0))
    summed = reduced(1, 0) + jnp.where(last == 0, 0.0, near)
    c3_copy(1).wait_recv()
    summed = summed + c3_in[1].astype(f32)
    c3_copy(0).wait_recv()
    summed = summed + c3_in[0].astype(f32)

    in_copies[5].wait()
    sig = jax.nn.sigmoid(summed)
    slope = up[...].astype(f32) * (sig * (1.0 + summed * (1.0 - sig)))

    def place(s, h, v, c):
        return ((c * Y + v) * 2 + s) * ZH + h

    kinds = ((0, zh), (1, zh), (0, ozh), (1, ozh))

    def tile(j, v, c):
        return slopes.at[place(*kinds[j], v, c)]

    slopes[place(0, zh, y, core)] = slope.T.astype(bf16)
    own, helps = tile(0, y, core), tile(1, y, core)
    turn = (ozh + last) % ZH
    e1 = (
        (own, own, (b, r_oz)),
        (own, helps, (b_up, r)),
        (
            slopes.at[place(0, turn, y, core)],
            slopes.at[place(1, turn, y, core)],
            (b_up, rep_of((zh + last) % ZH, y, core)),
        ),
    )

    def e1_copy(i):
        src, dst, dev = e1[i]
        return rc(src, dst, e1_s.at[i], e1_r.at[i], dev)

    def e2_copy(j, d, v):
        return rc(tile(j, v, core), tile(j, v, core), e2_s.at[j, d], e2_r.at[j, d], at_y(d))

    def e3_copy(j, d, c):
        got = tile(j, (y + Y - d) % Y, c)
        return rc(got, got, e3_s.at[j, d], e3_r.at[j, d], sib)

    def spread(j):
        for d in range(1, Y):
            go(e2_copy(j, d, y))
        go(e3_copy(j, 0, core))

    def pass_on(j):
        for d in range(1, Y):
            e2_copy(j, d, (y + Y - d) % Y).wait_recv()
            go(e3_copy(j, d, core))

    go(e1_copy(0))
    go(e1_copy(1))
    spread(0)
    hidden[...] = (summed * sig).astype(bf16)
    e1_copy(1).wait_recv()
    spread(1)
    pass_on(0)
    e1_copy(0).wait_recv()
    go(e1_copy(2))
    spread(2)
    pass_on(1)
    e1_copy(2).wait_recv()
    spread(3)
    for j in range(2, 4):
        pass_on(j)
    for j in range(4):
        for d in range(Y):
            e3_copy(j, d, 1 - core).wait_recv()

    def backward(n):
        out = None
        for s in range(2):
            q = s * SL + 2 * n
            lhs = jnp.concatenate(
                [slopes[table[6 + 2 * s, n]], slopes[table[7 + 2 * s, n]]], axis=1
            )
            term = dot(lhs, adj[pl.ds(q, 2)].reshape(2 * T, T))
            out = term if out is None else out + term
        out = out.astype(bf16)
        terms[n] = out
        return dot(out, feats[n])

    def gx_copy(k, e):
        first = ((x + e) % X) * ZL + (ohalf, half)[k] * ZQ
        return rc(terms.at[pl.ds(first, ZQ)], gx_in.at[k, e], gx_s.at[k, e], gx_r.at[k, e], at_x(e))

    total = jnp.zeros((T, T), f32)
    for k in range(2):
        for e in tuple(range(1, X)) + (0,):
            first = ((x + e) % X) * ZL + (ohalf, half)[k] * ZQ
            for i in range(ZQ):
                total = total + backward(first + i)
            if e:
                go(gx_copy(k, e))

    U = T // (2 * Y)
    wg_out[...] = total.reshape(2 * Y, U, T)

    def h0_copy():
        return rc(wg_out.at[pl.ds((1 - core) * Y, Y)], h0_in, h0_s, h0_r, sib)

    go(h0_copy())

    def gx_sum(k, v):
        t = terms[x * ZL + (ohalf, half)[k] * ZQ + v].astype(f32)
        for e in range(1, X):
            t = t + gx_in[k, e, v].astype(f32)
        return t

    def gz_copy(k, m):
        v = (zq + m) % ZQ
        return rc(
            gz_out.at[k, m],
            gz_in.at[k, m],
            gz_s.at[k, m],
            gz_r.at[k, m],
            (x * ZL + half * ZQ + v, r),
        )

    def gx_wait(k):
        for e in range(1, X):
            gx_copy(k, e).wait_recv()
        for m in range(1, ZQ):
            gz_out[k, m] = gx_sum(k, (zq + m) % ZQ).astype(bf16)
            go(gz_copy(k, m))
        return gx_sum(k, zq)

    def h1_copy(d):
        return rc(halves.at[(y + d) % Y], h1_in.at[d], h1_s.at[d], h1_r.at[d], at_y(d))

    h0_copy().wait_recv()
    halves[...] = wg_out[pl.ds(core * Y, Y)] + h0_in[...]
    for d in range(1, Y):
        go(h1_copy(d))

    crossing = gx_wait(0)

    zz = zh * ZL + z

    def h2_copy(i, to):
        h, d = (zh + i // ZL) % ZH, i % ZL
        v = (z + (d if to else ZL - d)) % ZL
        slot = h2_buf.at[zz] if to else h2_buf.at[h * ZL + v]
        dev = (x * ZL + v, rep_of(h, y, core))
        return rc(slot, slot, h2_s.at[i], h2_r.at[i], dev)

    unit = halves[y]
    for d in range(1, Y):
        h1_copy(d).wait_recv()
        unit = unit + h1_in[d]
    h2_buf[zz] = unit.astype(bf16)
    for i in range(1, ZH * ZL):
        go(h2_copy(i, True))

    kept = gx_wait(1)

    def gz2_copy():
        return rc(gz2_out, gz2_in, gz2_s, gz2_r, (x * ZL + ohalf * ZQ + zq, r))

    for m in range(1, ZQ):
        gz_copy(0, m).wait_recv()
        crossing = crossing + gz_in[0, m].astype(f32)
    gz2_out[...] = crossing.astype(bf16)
    go(gz2_copy())
    for m in range(1, ZQ):
        gz_copy(1, m).wait_recv()
        kept = kept + gz_in[1, m].astype(f32)

    def h3_copy(e, v):
        return rc(h3_buf.at[v], h3_buf.at[v], h3_s.at[e], h3_r.at[e], at_x(e))

    for i in range(1, ZH * ZL):
        h2_copy(i, False).wait_recv()
    unit = h2_buf[0].astype(f32)
    for i in range(1, ZH * ZL):
        unit = unit + h2_buf[i].astype(f32)
    h3_buf[x] = unit
    for e in range(1, X):
        go(h3_copy(e, x))

    gz2_copy().wait_recv()
    pulled = (kept + gz2_in[...].astype(f32)).T.astype(bf16)
    input_grad[...] = lax.dot_general(
        pulled, w, (((1,), (1,)), ((), ())), preferred_element_type=f32
    ).astype(bf16)

    def h4_copy(d, v):
        slot = wg_all.at[core * Y + v]
        return rc(slot, slot, h4_s.at[d], h4_r.at[d], at_y(d))

    def h5_copy(d, c):
        slot = wg_all.at[c * Y + (y + Y - d) % Y]
        return rc(slot, slot, h5_s.at[d], h5_r.at[d], sib)

    for e in range(1, X):
        h3_copy(e, (x + X - e) % X).wait_recv()
    unit = h3_buf[0]
    for e in range(1, X):
        unit = unit + h3_buf[e]
    wg_all[core * Y + y] = unit
    for d in range(1, Y):
        go(h4_copy(d, y))
    go(h5_copy(0, core))
    for d in range(1, Y):
        h4_copy(d, (y + Y - d) % Y).wait_recv()
        go(h5_copy(d, core))
    for d in range(Y):
        h5_copy(d, 1 - core).wait_recv()
    weight_grad[...] = wg_all[...].reshape(T, T).T

    for copy in sends:
        copy.wait_send()


def local(features, weight, adjacency, row_tiles, live_counts, upstream):
    BLK, REP = X * ZL, ZH * Y * 2
    f32, bf16 = jnp.float32, jnp.bfloat16
    adj = adjacency.reshape(4 * BLK, T, T)
    rows = jnp.swapaxes(row_tiles, 3, 4).reshape(2, 2, BLK)
    live = live_counts.reshape(2, BLK)
    vmem = pl.BlockSpec(memory_space=pltpu.VMEM)

    def buf(*dims, dtype=bf16):
        return pltpu.VMEM(dims + (T,), dtype)

    U = T // (2 * Y)
    dma = pltpu.SemaphoreType.DMA
    scratch = [
        buf(4 * BLK, T),
        buf(T),
        buf(T),
        pltpu.VMEM((2, 2, BLK), jnp.int32),
        pltpu.VMEM((2, BLK), jnp.int32),
        buf(16, dtype=jnp.int32),
        pltpu.SMEM((16, T), jnp.int32),
        buf(BLK, T),
        buf(4 * BLK + 1, T, dtype=f32),
        buf(2, Y, 2, T),
        buf(2, Y, 2, T),
        buf(2, Y, 2, T),
        buf(2, Y, 2, T),
        buf(2, 2, T, dtype=f32),
        buf(3, T),
        buf(3, T),
        buf(2 * REP + 1, T),
        buf(BLK, T),
        buf(2, X, ZQ, T),
        buf(2, ZQ, T),
        buf(2, ZQ, T),
        buf(T),
        buf(T),
        buf(2 * Y, U, dtype=f32),
        buf(Y, U, dtype=f32),
        buf(Y, U, dtype=f32),
        buf(Y, U, dtype=f32),
        buf(ZH * ZL, U),
        buf(X, U, dtype=f32),
        buf(2 * Y, U, dtype=f32),
        dma((7,)),
        dma((ZL,)),
        dma((ZL,)),
        dma((X, ZL)),
        dma((X, ZL)),
        dma((2, Y)),
        dma((2, Y)),
        dma((2, Y)),
        dma((2, Y)),
        dma((3,)),
        dma((3,)),
        dma((3,)),
        dma((3,)),
        dma((4, Y)),
        dma((4, Y)),
        dma((4, Y)),
        dma((4, Y)),
        dma((2, X)),
        dma((2, X)),
        dma((2, ZQ)),
        dma((2, ZQ)),
        dma,
        dma,
        dma,
        dma,
        dma((Y,)),
        dma((Y,)),
        dma((ZH * ZL,)),
        dma((ZH * ZL,)),
        dma((X,)),
        dma((X,)),
        dma((Y,)),
        dma((Y,)),
        dma((Y,)),
        dma((Y,)),
    ]
    return pl.pallas_call(
        kernel,
        name="graph_layer",
        out_shape=(
            jax.ShapeDtypeStruct((T, T), bf16),
            jax.ShapeDtypeStruct((T, T), bf16),
            jax.ShapeDtypeStruct((T, T), f32),
        ),
        in_specs=[pl.BlockSpec(memory_space=pltpu.HBM)] * 6,
        out_specs=(vmem, vmem, vmem),
        scratch_shapes=scratch,
        compiler_params=pltpu.CompilerParams(
            collective_id=0, has_side_effects=True, vmem_limit_bytes=64 * 1024 * 1024
        ),
    )(features, weight, upstream, adj, rows, live)


def solution(mesh):
    assert mesh.shape["blk"] == X * ZL and mesh.shape["rep"] == ZH * Y * 2
    in_specs = (
        P(("blk", "rep"), None),
        P(),
        P("blk", "rep", None, None, None, None, None),
        P("blk", "rep", None, None, None),
        P("blk", "rep", None, None),
        P(("blk", "rep"), None),
    )
    out_specs = (P(("blk", "rep"), None), P(("blk", "rep"), None), P())
    return jax.shard_map(local, mesh=mesh, in_specs=in_specs, out_specs=out_specs, check_vma=False)
```

```python
import functools

import jax
import jax.numpy as jnp
from jax import lax
from jax.experimental import pallas as pl
from jax.experimental.pallas import tpu as pltpu
from jax.sharding import PartitionSpec as P

MESH = pl.DeviceIdType.MESH
X, ZL, ZH, Y = 4, 8, 2, 4
ZQ = ZL // 2
T = 128


def dot(a, b):
    return jnp.dot(a, b, preferred_element_type=jnp.float32)


def kernel(
    feat_hbm,
    weight_hbm,
    up_hbm,
    adj_hbm,
    rows_hbm,
    live_hbm,
    hidden,
    input_grad,
    weight_grad,
    adj,
    up,
    up_far,
    weight,
    rows_v,
    live_v,
    tab_v,
    table,
    feats,
    sums,
    c1_out,
    c1_in,
    c2_out,
    c2_in,
    part,
    c3_out,
    c3_in,
    slopes,
    terms,
    gx_in,
    gz_out,
    gz_in,
    gz2_out,
    gz2_in,
    wg_out,
    h0_in,
    halves,
    h1_in,
    h2_buf,
    h3_buf,
    wg_all,
    in_sem,
    az_s,
    az_r,
    ax_s,
    ax_r,
    up_s,
    up_r,
    c1_s,
    c1_r,
    c2_s,
    c2_r,
    c3_s,
    c3_r,
    e2_s,
    e2_r,
    e3_s,
    e3_r,
    gx_s,
    gx_r,
    gz_s,
    gz_r,
    gz2_s,
    gz2_r,
    h0_s,
    h0_r,
    h1_s,
    h1_r,
    h2_s,
    h2_r,
    h3_s,
    h3_r,
    h4_s,
    h4_r,
    h5_s,
    h5_r,
):
    BLK, REP = X * ZL, ZH * Y * 2
    SL = 2 * BLK
    f32, bf16 = jnp.float32, jnp.bfloat16
    b = lax.axis_index("blk")
    r = lax.axis_index("rep")
    x, z = b // ZL, b % ZL
    zh, y, core = r // (2 * Y), (r // 2) % Y, r % 2
    ozh = (zh + 1) % ZH
    b_up, b_dn = (b + 1) % BLK, (b + BLK - 1) % BLK

    def at_z(d):
        return (x * ZL + (z + d) % ZL, r)

    def at_x(d):
        return (((x + d) % X) * ZL + z, r)

    def rep_of(h, v, c):
        return (h * Y + v) * 2 + c

    def at_y(d):
        return (b, rep_of(zh, (y + d) % Y, core))

    first, last = (ZL - z) // ZL, (z + 1) // ZL

    def at_dn(d):
        return (b_dn, rep_of((zh + first) % ZH, (y + d) % Y, core))

    def at_up(d):
        return (b_up, rep_of((zh + last) % ZH, (y + d) % Y, core))

    sib = (b, rep_of(zh, y, 1 - core))
    r_oz = rep_of(ozh, y, core)

    def rc(src, dst, ss, rs, dev):
        return pltpu.make_async_remote_copy(
            src_ref=src, dst_ref=dst, send_sem=ss, recv_sem=rs, device_id=dev, device_id_type=MESH
        )

    in_copies = [
        pltpu.make_async_copy(src, dst, in_sem.at[i])
        for i, (src, dst) in enumerate(
            (
                (feat_hbm, feats.at[b]),
                (rows_hbm, rows_v),
                (live_hbm, live_v),
                (weight_hbm, weight),
                (adj_hbm, adj),
                (up_hbm, up),
            )
        )
    ]
    for copy in in_copies:
        copy.start()

    bar = pltpu.get_barrier_semaphore()

    def greet(dev):
        pl.semaphore_signal(bar, inc=1, device_id=dev, device_id_type=MESH)

    for i in range(1, ZH * ZL):
        greet((x * ZL + (z + i % ZL) % ZL, rep_of((zh + i // ZL) % ZH, y, core)))
    for d in range(1, X):
        greet(at_x(d))
    for d in range(1, Y):
        greet(at_y(d))
    greet(sib)
    for d in range(Y):
        greet(at_up(d))
        greet(at_dn(d))

    half, zq = z // ZQ, z % ZQ
    ohalf = 1 - half

    in_copies[1].wait()
    in_copies[2].wait()
    i_s = lax.broadcasted_iota(jnp.int32, (BLK, BLK), 0)
    i_l = lax.broadcasted_iota(jnp.int32, (BLK, BLK), 1)

    def rank(n):
        far = ((n // ZQ) % 2) ^ half
        return (far * ZQ + ((zq - n % ZQ) & (ZQ - 1))) * X + ((x - n // ZL) & (X - 1))

    rank_s, rank_l = rank(i_s), rank(i_l)

    def to_rows(lanes):
        return jnp.sum(jnp.where(i_s == i_l, lanes, 0), axis=1, keepdims=True)

    t_l = lax.broadcasted_iota(jnp.int32, (BLK, REP), 1)
    for s in range(2):
        row_s = [to_rows(rows_v[s, k : k + 1, :]) for k in range(2)]
        live_l = live_v[s : s + 1, :]
        live_s = to_rows(live_l)
        code = [(2 * rank_s + k) * 1024 + s * SL + 2 * i_s + k for k in range(2)]

        def best(hits):
            found = jnp.max(jnp.maximum(hits[0], hits[1]), axis=0, keepdims=True)
            return jnp.where(found < 0, 2 * SL, found & 1023)

        for k in range(2):
            row_l = rows_v[s, k : k + 1, :]
            hits = [
                jnp.where(
                    (row_s[o] == row_l) & (live_s > o) & (2 * rank_s + o < 2 * rank_l + k),
                    code[o],
                    -1,
                )
                for o in range(2)
            ]
            tab_v[2 * s + k : 2 * s + k + 1, :BLK] = best(hits)
            spot = ((((row_l & 1) * Y + ((row_l // 2) & (Y - 1))) * 2 + s) * ZH) + row_l // (2 * Y)
            tab_v[6 + 2 * s + k : 7 + 2 * s + k, :BLK] = jnp.where(live_l > k, spot, 2 * REP)
        hits = [
            jnp.where((row_s[o] == t_l) & (live_s > o), code[o][:, :1], -1) for o in range(2)
        ]
        tab_v[4 + s : 5 + s, :REP] = best(hits)
    to_scalars = pltpu.make_async_copy(tab_v, table, in_sem.at[6])
    to_scalars.start()
    sums[2 * SL] = jnp.zeros((T, T), f32)
    slopes[2 * REP] = jnp.zeros((T, T), bf16)
    in_copies[0].wait()
    in_copies[3].wait()

    sends = []

    def go(copy):
        copy.start()
        sends.append(copy)
        return copy

    pl.semaphore_wait(bar, (ZH * ZL - 1) + (X - 1) + (Y - 1) + 1 + 2 * Y)

    def zsrc(g):
        return (half, ohalf)[g // ZQ] * ZQ + (zq + ZQ - g % ZQ) % ZQ

    def mate(m):
        return (x * ZL + half * ZQ + (zq + m) % ZQ, r)

    partner = (x * ZL + ohalf * ZQ + zq, r)

    def az_copy(g, v, dev):
        slot = feats.at[x * ZL + v]
        return rc(slot, slot, az_s.at[g], az_r.at[g], dev)

    def ax_copy(g, e, v):
        slot = feats.at[v * ZL + zsrc(g)]
        return rc(slot, slot, ax_s.at[e, g], ax_r.at[e, g], at_x(e))

    def along_x(g):
        for e in range(1, X):
            go(ax_copy(g, e, x))

    go(az_copy(ZQ, z, partner))
    for m in range(1, ZQ):
        go(az_copy(m, z, mate(m)))
    along_x(0)
    for m in range(1, ZQ):
        az_copy(m, zsrc(m), mate(m)).wait_recv()
        along_x(m)
    az_copy(ZQ, zsrc(ZQ), partner).wait_recv()
    for m in range(1, ZQ):
        go(az_copy(ZQ + m, zsrc(ZQ), mate(m)))
    along_x(ZQ)
    in_copies[4].wait()
    to_scalars.wait()

    w = weight[...]

    def forward(g):
        for e in range(X):
            v = (x + X - e) % X
            if e:
                ax_copy(g, e, v).wait_recv()
            n = v * ZL + zsrc(g)
            mixed = dot(feats[n], w).astype(bf16)
            for s in range(2):
                q = s * SL + 2 * n
                prod = dot(adj[pl.ds(q, 2)].reshape(2 * T, T), mixed)
                sums[q] = prod[:T] + sums[table[2 * s, n]]
                sums[q + 1] = prod[T:] + sums[table[2 * s + 1, n]]

    early = ZQ - 1
    for g in range(early):
        forward(g)
    for m in range(1, ZQ):
        az_copy(ZQ + m, zsrc(ZQ + m), mate(m)).wait_recv()
        along_x(ZQ + m)
    for g in range(early, ZL):
        forward(g)

    def routed(s, t):
        return sums[table[4 + s, t]]

    def up_copy():
        return rc(up, up_far, up_s, up_r, (b, r_oz))

    in_copies[5].wait()
    go(up_copy())
    order = tuple(range(1, Y)) + (0,)

    def c1_copy(d):
        return rc(c1_out.at[d], c1_in.at[d], c1_s.at[d], c1_r.at[d], sib)

    def c2_copy(s, d):
        dev = at_dn(d) if s else at_y(d)
        return rc(c2_out.at[s, d], c2_in.at[s, d], c2_s.at[s, d], c2_r.at[s, d], dev)

    for d in order:
        for s in range(2):
            for h in range(ZH):
                c1_out[d, s, h] = routed(s, rep_of(h, (y + d) % Y, 1 - core)).astype(bf16)
        go(c1_copy(d))
    for d in order:
        c1_copy(d).wait_recv()
        for s in (1, 0):
            for h in range(ZH):
                both = routed(s, rep_of(h, (y + d) % Y, core)) + c1_in[d, s, h].astype(f32)
                if s or d:
                    c2_out[s, d, h] = both.astype(bf16)
                else:
                    part[h] = both
            if s or d:
                go(c2_copy(s, d))

    for s in range(2):
        for d in range(1 - s, Y):
            c2_copy(s, d).wait_recv()
    for h in range(ZH):
        t = part[h]
        for s in range(2):
            for d in range(1 - s, Y):
                t = t + c2_in[s, d, h].astype(f32)
        part[h] = t
        c3_out[h] = t.astype(bf16)

    def c3_copy():
        return rc(c3_out, c3_in, c3_s, c3_r, (b, r_oz))

    go(c3_copy())
    up_copy().wait_recv()
    c3_copy().wait_recv()

    def place(s, h, v, c):
        return ((c * Y + v) * 2 + s) * ZH + h

    for h in range(ZH):
        summed = part[h] + c3_in[h].astype(f32)
        sig = jax.nn.sigmoid(summed)
        given = jnp.where(zh == h, up[...], up_far[...]).astype(f32)
        slope = given * (sig * (1.0 + summed * (1.0 - sig)))
        slopes[place(0, h, y, core)] = slope.T.astype(bf16)
        part[h] = summed * sig

    def pair(s, v, c):
        return slopes.at[pl.ds(place(s, 0, v, c), ZH)]

    def e2_copy(s, d):
        dev = at_up(d) if s else at_y(d)
        own = pair(0, y, core)
        return rc(own, pair(s, y, core), e2_s.at[s, d], e2_r.at[s, d], dev)

    def e3_copy(s, d, c):
        got = pair(s, (y + Y - d) % Y, c)
        return rc(got, got, e3_s.at[s, d], e3_r.at[s, d], sib)

    for d in order:
        go(e2_copy(1, d))
        if d:
            go(e2_copy(0, d))
    go(e3_copy(0, 0, core))
    hidden[...] = part[zh].astype(bf16)
    for d in (0,) + order[:-1]:
        for s in range(2):
            if s or d:
                e2_copy(s, d).wait_recv()
                go(e3_copy(s, d, core))
    for s in range(2):
        for d in range(Y):
            e3_copy(s, d, 1 - core).wait_recv()

    def backward(n):
        out = None
        for s in range(2):
            q = s * SL + 2 * n
            lhs = jnp.concatenate(
                [slopes[table[6 + 2 * s, n]], slopes[table[7 + 2 * s, n]]], axis=1
            )
            term = dot(lhs, adj[pl.ds(q, 2)].reshape(2 * T, T))
            out = term if out is None else out + term
        out = out.astype(bf16)
        terms[n] = out
        return dot(out, feats[n])

    def gx_copy(k, e):
        first = ((x + e) % X) * ZL + (ohalf, half)[k] * ZQ
        return rc(terms.at[pl.ds(first, ZQ)], gx_in.at[k, e], gx_s.at[k, e], gx_r.at[k, e], at_x(e))

    total = jnp.zeros((T, T), f32)
    for k in range(2):
        for e in tuple(range(1, X)) + (0,):
            first = ((x + e) % X) * ZL + (ohalf, half)[k] * ZQ
            for i in range(ZQ):
                total = total + backward(first + i)
            if e:
                go(gx_copy(k, e))

    U = T // (2 * Y)
    wg_out[...] = total.reshape(2 * Y, U, T)

    def h0_copy():
        return rc(wg_out.at[pl.ds((1 - core) * Y, Y)], h0_in, h0_s, h0_r, sib)

    go(h0_copy())

    def gx_sum(k, v):
        t = terms[x * ZL + (ohalf, half)[k] * ZQ + v].astype(f32)
        for e in range(1, X):
            t = t + gx_in[k, e, v].astype(f32)
        return t

    def gz_copy(k, m):
        v = (zq + m) % ZQ
        return rc(
            gz_out.at[k, m],
            gz_in.at[k, m],
            gz_s.at[k, m],
            gz_r.at[k, m],
            (x * ZL + half * ZQ + v, r),
        )

    def gx_wait(k):
        for e in range(1, X):
            gx_copy(k, e).wait_recv()
        for m in range(1, ZQ):
            gz_out[k, m] = gx_sum(k, (zq + m) % ZQ).astype(bf16)
            go(gz_copy(k, m))
        return gx_sum(k, zq)

    def h1_copy(d):
        return rc(halves.at[(y + d) % Y], h1_in.at[d], h1_s.at[d], h1_r.at[d], at_y(d))

    h0_copy().wait_recv()
    halves[...] = wg_out[pl.ds(core * Y, Y)] + h0_in[...]
    for d in range(1, Y):
        go(h1_copy(d))

    crossing = gx_wait(0)

    zz = zh * ZL + z

    def h2_copy(i, to):
        h, d = (zh + i // ZL) % ZH, i % ZL
        v = (z + (d if to else ZL - d)) % ZL
        slot = h2_buf.at[zz] if to else h2_buf.at[h * ZL + v]
        dev = (x * ZL + v, rep_of(h, y, core))
        return rc(slot, slot, h2_s.at[i], h2_r.at[i], dev)

    unit = halves[y]
    for d in range(1, Y):
        h1_copy(d).wait_recv()
        unit = unit + h1_in[d]
    h2_buf[zz] = unit.astype(bf16)
    for i in range(1, ZH * ZL):
        go(h2_copy(i, True))

    kept = gx_wait(1)

    def gz2_copy():
        return rc(gz2_out, gz2_in, gz2_s, gz2_r, (x * ZL + ohalf * ZQ + zq, r))

    for m in range(1, ZQ):
        gz_copy(0, m).wait_recv()
        crossing = crossing + gz_in[0, m].astype(f32)
    gz2_out[...] = crossing.astype(bf16)
    go(gz2_copy())
    for m in range(1, ZQ):
        gz_copy(1, m).wait_recv()
        kept = kept + gz_in[1, m].astype(f32)

    def h3_copy(e, v):
        return rc(h3_buf.at[v], h3_buf.at[v], h3_s.at[e], h3_r.at[e], at_x(e))

    for i in range(1, ZH * ZL):
        h2_copy(i, False).wait_recv()
    unit = h2_buf[0].astype(f32)
    for i in range(1, ZH * ZL):
        unit = unit + h2_buf[i].astype(f32)
    h3_buf[x] = unit
    for e in range(1, X):
        go(h3_copy(e, x))

    gz2_copy().wait_recv()
    pulled = (kept + gz2_in[...].astype(f32)).T.astype(bf16)
    input_grad[...] = lax.dot_general(
        pulled, w, (((1,), (1,)), ((), ())), preferred_element_type=f32
    ).astype(bf16)

    def h4_copy(d, v):
        slot = wg_all.at[core * Y + v]
        return rc(slot, slot, h4_s.at[d], h4_r.at[d], at_y(d))

    def h5_copy(d, c):
        slot = wg_all.at[c * Y + (y + Y - d) % Y]
        return rc(slot, slot, h5_s.at[d], h5_r.at[d], sib)

    for e in range(1, X):
        h3_copy(e, (x + X - e) % X).wait_recv()
    unit = h3_buf[0]
    for e in range(1, X):
        unit = unit + h3_buf[e]
    wg_all[core * Y + y] = unit
    for d in range(1, Y):
        go(h4_copy(d, y))
    go(h5_copy(0, core))
    for d in range(1, Y):
        h4_copy(d, (y + Y - d) % Y).wait_recv()
        go(h5_copy(d, core))
    for d in range(Y):
        h5_copy(d, 1 - core).wait_recv()
    weight_grad[...] = wg_all[...].reshape(T, T).T

    for copy in sends:
        copy.wait_send()


def local(features, weight, adjacency, row_tiles, live_counts, upstream):
    BLK, REP = X * ZL, ZH * Y * 2
    f32, bf16 = jnp.float32, jnp.bfloat16
    adj = adjacency.reshape(4 * BLK, T, T)
    rows = jnp.swapaxes(row_tiles, 3, 4).reshape(2, 2, BLK)
    live = live_counts.reshape(2, BLK)
    vmem = pl.BlockSpec(memory_space=pltpu.VMEM)

    def buf(*dims, dtype=bf16):
        return pltpu.VMEM(dims + (T,), dtype)

    U = T // (2 * Y)
    dma = pltpu.SemaphoreType.DMA
    scratch = [
        buf(4 * BLK, T),
        buf(T),
        buf(T),
        buf(T),
        pltpu.VMEM((2, 2, BLK), jnp.int32),
        pltpu.VMEM((2, BLK), jnp.int32),
        buf(16, dtype=jnp.int32),
        pltpu.SMEM((16, T), jnp.int32),
        buf(BLK, T),
        buf(4 * BLK + 1, T, dtype=f32),
        buf(Y, 2, ZH, T),
        buf(Y, 2, ZH, T),
        buf(2, Y, ZH, T),
        buf(2, Y, ZH, T),
        buf(ZH, T, dtype=f32),
        buf(ZH, T),
        buf(ZH, T),
        buf(2 * REP + 1, T),
        buf(BLK, T),
        buf(2, X, ZQ, T),
        buf(2, ZQ, T),
        buf(2, ZQ, T),
        buf(T),
        buf(T),
        buf(2 * Y, U, dtype=f32),
        buf(Y, U, dtype=f32),
        buf(Y, U, dtype=f32),
        buf(Y, U, dtype=f32),
        buf(ZH * ZL, U),
        buf(X, U, dtype=f32),
        buf(2 * Y, U, dtype=f32),
        dma((7,)),
        dma((ZL,)),
        dma((ZL,)),
        dma((X, ZL)),
        dma((X, ZL)),
        dma,
        dma,
        dma((Y,)),
        dma((Y,)),
        dma((2, Y)),
        dma((2, Y)),
        dma,
        dma,
        dma((2, Y)),
        dma((2, Y)),
        dma((2, Y)),
        dma((2, Y)),
        dma((2, X)),
        dma((2, X)),
        dma((2, ZQ)),
        dma((2, ZQ)),
        dma,
        dma,
        dma,
        dma,
        dma((Y,)),
        dma((Y,)),
        dma((ZH * ZL,)),
        dma((ZH * ZL,)),
        dma((X,)),
        dma((X,)),
        dma((Y,)),
        dma((Y,)),
        dma((Y,)),
        dma((Y,)),
    ]
    return pl.pallas_call(
        kernel,
        name="graph_layer",
        out_shape=(
            jax.ShapeDtypeStruct((T, T), bf16),
            jax.ShapeDtypeStruct((T, T), bf16),
            jax.ShapeDtypeStruct((T, T), f32),
        ),
        in_specs=[pl.BlockSpec(memory_space=pltpu.HBM)] * 6,
        out_specs=(vmem, vmem, vmem),
        scratch_shapes=scratch,
        compiler_params=pltpu.CompilerParams(
            collective_id=0, has_side_effects=True, vmem_limit_bytes=48 * 1024 * 1024
        ),
    )(
        *(
            pltpu.with_memory_space_constraint(v, pltpu.HBM)
            for v in (features, weight, upstream, adj, rows, live)
        )
    )


def solution(mesh):
    assert mesh.shape["blk"] == X * ZL and mesh.shape["rep"] == ZH * Y * 2
    in_specs = (
        P(("blk", "rep"), None),
        P(),
        P("blk", "rep", None, None, None, None, None),
        P("blk", "rep", None, None, None),
        P("blk", "rep", None, None),
        P(("blk", "rep"), None),
    )
    out_specs = (P(("blk", "rep"), None), P(("blk", "rep"), None), P())
    return jax.shard_map(local, mesh=mesh, in_specs=in_specs, out_specs=out_specs, check_vma=False)
```

```python
import functools

import jax
import jax.numpy as jnp
from jax import lax
from jax.experimental import pallas as pl
from jax.experimental.pallas import tpu as pltpu
from jax.sharding import PartitionSpec as P

MESH = pl.DeviceIdType.MESH
X, ZL, ZH, Y = 4, 8, 2, 4
ZQ = ZL // 2
T = 128


def dot(a, b):
    return jnp.dot(a, b, preferred_element_type=jnp.float32)


def kernel(
    feat_hbm,
    weight_hbm,
    up_hbm,
    adj_hbm,
    rows_hbm,
    live_hbm,
    hidden,
    input_grad,
    weight_grad,
    adj,
    up,
    up_far,
    weight,
    rows_v,
    live_v,
    tab_v,
    table,
    feats,
    sums,
    c1_out,
    c1_in,
    c2_out,
    c2_in,
    part,
    c3_out,
    c3_in,
    tops,
    slopes,
    terms,
    gx_in,
    gz_out,
    gz_in,
    gz2_out,
    gz2_in,
    wg_out,
    h0_in,
    halves,
    h1_in,
    h2_buf,
    h3_buf,
    wg_all,
    in_sem,
    az_s,
    az_r,
    ax_s,
    ax_r,
    up_s,
    up_r,
    c1_s,
    c1_r,
    c2_s,
    c2_r,
    c3_s,
    c3_r,
    e2_s,
    e2_r,
    e3_s,
    e3_r,
    gx_s,
    gx_r,
    gz_s,
    gz_r,
    gz2_s,
    gz2_r,
    h0_s,
    h0_r,
    h1_s,
    h1_r,
    h2_s,
    h2_r,
    h3_s,
    h3_r,
    h4_s,
    h4_r,
    h5_s,
    h5_r,
):
    BLK, REP = X * ZL, ZH * Y * 2
    SL = 2 * BLK
    f32, bf16 = jnp.float32, jnp.bfloat16
    b = lax.axis_index("blk")
    r = lax.axis_index("rep")
    x, z = b // ZL, b % ZL
    zh, y, core = r // (2 * Y), (r // 2) % Y, r % 2
    ozh = (zh + 1) % ZH
    b_up, b_dn = (b + 1) % BLK, (b + BLK - 1) % BLK

    def at_z(d):
        return (x * ZL + (z + d) % ZL, r)

    def at_x(d):
        return (((x + d) % X) * ZL + z, r)

    def rep_of(h, v, c):
        return (h * Y + v) * 2 + c

    def at_y(d):
        return (b, rep_of(zh, (y + d) % Y, core))

    first, last = (ZL - z) // ZL, (z + 1) // ZL

    def at_dn(d):
        return (b_dn, rep_of((zh + first) % ZH, (y + d) % Y, core))

    def at_up(d):
        return (b_up, rep_of((zh + last) % ZH, (y + d) % Y, core))

    sib = (b, rep_of(zh, y, 1 - core))
    r_oz = rep_of(ozh, y, core)

    def rc(src, dst, ss, rs, dev):
        return pltpu.make_async_remote_copy(
            src_ref=src, dst_ref=dst, send_sem=ss, recv_sem=rs, device_id=dev, device_id_type=MESH
        )

    in_copies = [
        pltpu.make_async_copy(src, dst, in_sem.at[i])
        for i, (src, dst) in enumerate(
            (
                (feat_hbm, feats.at[b]),
                (rows_hbm, rows_v),
                (live_hbm, live_v),
                (weight_hbm, weight),
                (adj_hbm, adj),
                (up_hbm, up),
            )
        )
    ]
    for copy in in_copies:
        copy.start()

    bar = pltpu.get_barrier_semaphore()

    def greet(dev):
        pl.semaphore_signal(bar, inc=1, device_id=dev, device_id_type=MESH)

    for i in range(1, ZH * ZL):
        greet((x * ZL + (z + i % ZL) % ZL, rep_of((zh + i // ZL) % ZH, y, core)))
    for d in range(1, X):
        greet(at_x(d))
    for d in range(1, Y):
        greet(at_y(d))
    greet(sib)
    for d in range(Y):
        greet(at_up(d))
        greet(at_dn(d))

    half, zq = z // ZQ, z % ZQ
    ohalf = 1 - half

    in_copies[1].wait()
    in_copies[2].wait()
    i_s = lax.broadcasted_iota(jnp.int32, (BLK, BLK), 0)
    i_l = lax.broadcasted_iota(jnp.int32, (BLK, BLK), 1)

    def rank(n):
        far = ((n // ZQ) % 2) ^ half
        return (far * ZQ + ((zq - n % ZQ) & (ZQ - 1))) * X + ((x - n // ZL) & (X - 1))

    rank_s, rank_l = rank(i_s), rank(i_l)

    def to_rows(lanes):
        return jnp.sum(jnp.where(i_s == i_l, lanes, 0), axis=1, keepdims=True)

    t_l = lax.broadcasted_iota(jnp.int32, (BLK, REP), 1)
    for s in range(2):
        row_s = [to_rows(rows_v[s, k : k + 1, :]) for k in range(2)]
        live_l = live_v[s : s + 1, :]
        live_s = to_rows(live_l)
        code = [(2 * rank_s + k) * 1024 + s * SL + 2 * i_s + k for k in range(2)]

        def best(hits):
            found = jnp.max(jnp.maximum(hits[0], hits[1]), axis=0, keepdims=True)
            return jnp.where(found < 0, 2 * SL, found & 1023)

        for k in range(2):
            row_l = rows_v[s, k : k + 1, :]
            hits = [
                jnp.where(
                    (row_s[o] == row_l) & (live_s > o) & (2 * rank_s + o < 2 * rank_l + k),
                    code[o],
                    -1,
                )
                for o in range(2)
            ]
            tab_v[2 * s + k : 2 * s + k + 1, :BLK] = best(hits)
            spot = ((((row_l & 1) * Y + ((row_l // 2) & (Y - 1))) * 2 + s) * ZH) + row_l // (2 * Y)
            tab_v[6 + 2 * s + k : 7 + 2 * s + k, :BLK] = jnp.where(live_l > k, spot, 2 * REP)
        hits = [
            jnp.where((row_s[o] == t_l) & (live_s > o), code[o][:, :1], -1) for o in range(2)
        ]
        tab_v[4 + s : 5 + s, :REP] = best(hits)
    to_scalars = pltpu.make_async_copy(tab_v, table, in_sem.at[6])
    to_scalars.start()
    sums[2 * SL] = jnp.zeros((T, T), f32)
    slopes[2 * REP] = jnp.zeros((T, T), bf16)
    in_copies[0].wait()
    in_copies[3].wait()

    sends = []

    def go(copy):
        copy.start()
        sends.append(copy)
        return copy

    def flush(keep):
        done = sends[: len(sends) - keep]
        del sends[: len(done)]
        for copy in done:
            copy.wait_send()

    pl.semaphore_wait(bar, (ZH * ZL - 1) + (X - 1) + (Y - 1) + 1 + 2 * Y)

    def zsrc(g):
        return (half, ohalf)[g // ZQ] * ZQ + (zq + ZQ - g % ZQ) % ZQ

    def mate(m):
        return (x * ZL + half * ZQ + (zq + m) % ZQ, r)

    partner = (x * ZL + ohalf * ZQ + zq, r)

    def az_copy(g, v, dev):
        slot = feats.at[x * ZL + v]
        return rc(slot, slot, az_s.at[g], az_r.at[g], dev)

    def ax_copy(g, e, v):
        slot = feats.at[v * ZL + zsrc(g)]
        return rc(slot, slot, ax_s.at[e, g], ax_r.at[e, g], at_x(e))

    def along_x(g):
        for e in range(1, X):
            go(ax_copy(g, e, x))

    go(az_copy(ZQ, z, partner))
    for m in range(1, ZQ):
        go(az_copy(m, z, mate(m)))
    along_x(0)
    for m in range(1, ZQ):
        az_copy(m, zsrc(m), mate(m)).wait_recv()
        along_x(m)
    az_copy(ZQ, zsrc(ZQ), partner).wait_recv()
    for m in range(1, ZQ):
        go(az_copy(ZQ + m, zsrc(ZQ), mate(m)))
    along_x(ZQ)
    in_copies[4].wait()
    to_scalars.wait()


    def forward(g):
        for e in range(X):
            v = (x + X - e) % X
            if e:
                ax_copy(g, e, v).wait_recv()
            n = v * ZL + zsrc(g)
            for s in range(2):
                q = s * SL + 2 * n
                prod = dot(adj[pl.ds(q, 2)].reshape(2 * T, T), feats[n])
                sums[q] = prod[:T] + sums[table[2 * s, n]]
                sums[q + 1] = prod[T:] + sums[table[2 * s + 1, n]]

    early = ZQ - 1
    for g in range(early):
        forward(g)
    for m in range(1, ZQ):
        az_copy(ZQ + m, zsrc(ZQ + m), mate(m)).wait_recv()
        along_x(ZQ + m)
    for g in range(early, ZL):
        forward(g)

    def routed(s, t):
        return sums[table[4 + s, t]]

    def up_copy():
        return rc(up, up_far, up_s, up_r, (b, r_oz))

    in_copies[5].wait()
    go(up_copy())
    order = tuple(range(1, Y)) + (0,)

    def c1_copy(h, d):
        return rc(c1_out.at[h, d], c1_in.at[h, d], c1_s.at[h, d], c1_r.at[h, d], sib)

    def c2_copy(h, s, d):
        dev = at_dn(d) if s else at_y(d)
        i = (h, s, d)
        return rc(c2_out.at[i], c2_in.at[i], c2_s.at[i], c2_r.at[i], dev)

    def c3_copy(h):
        return rc(c3_out.at[h], c3_in.at[h], c3_s.at[h], c3_r.at[h], (b, r_oz))

    for h in range(ZH):
        for d in order:
            for s in range(2):
                c1_out[h, d, s] = routed(s, rep_of(h, (y + d) % Y, 1 - core)).astype(bf16)
            go(c1_copy(h, d))
    for h in range(ZH):
        for d in order:
            c1_copy(h, d).wait_recv()
            for s in (1, 0):
                both = routed(s, rep_of(h, (y + d) % Y, core)) + c1_in[h, d, s].astype(f32)
                if s or d:
                    c2_out[h, s, d] = both.astype(bf16)
                    go(c2_copy(h, s, d))
                else:
                    part[h] = both
    for h in range(ZH):
        t = part[h]
        for s in range(2):
            for d in range(1 - s, Y):
                c2_copy(h, s, d).wait_recv()
                t = t + c2_in[h, s, d].astype(f32)
        part[h] = t
        c3_out[h] = t.astype(bf16)
        go(c3_copy(h))
    flush(ZH)
    up_copy().wait_recv()

    def place(s, h, v, c):
        return ((c * Y + v) * 2 + s) * ZH + h

    def tile(s, h, v, c):
        return slopes.at[place(s, h, v, c)]

    def e2_copy(h, s, d):
        dev = at_up(d) if s else at_y(d)
        own = tile(0, h, y, core)
        return rc(own, tile(s, h, y, core), e2_s.at[h, s, d], e2_r.at[h, s, d], dev)

    def e3_copy(h, s, d, c):
        got = tile(s, h, (y + Y - d) % Y, c)
        return rc(got, got, e3_s.at[h, s, d], e3_r.at[h, s, d], sib)

    w = weight[...]
    for h in range(ZH):
        c3_copy(h).wait_recv()
        gathered = part[h] + c3_in[h].astype(f32)
        high = gathered.astype(bf16)
        low = (gathered - high.astype(f32)).astype(bf16)
        tops[h] = high
        summed = dot(high, w) + dot(low, w)
        sig = jax.nn.sigmoid(summed)
        given = jnp.where(zh == h, up[...], up_far[...]).astype(f32)
        slope = given * (sig * (1.0 + summed * (1.0 - sig)))
        slopes[place(0, h, y, core)] = slope.T.astype(bf16)
        for d in order:
            go(e2_copy(h, 1, d))
            if d:
                go(e2_copy(h, 0, d))
        go(e3_copy(h, 0, 0, core))
        part[h] = summed * sig
    hidden[...] = part[zh].astype(bf16)

    U = T // (2 * Y)
    total = dot(slopes[place(0, zh, y, core)], tops[zh])
    wg_out[...] = total.reshape(2 * Y, U, T)

    def h0_copy():
        return rc(wg_out.at[pl.ds((1 - core) * Y, Y)], h0_in, h0_s, h0_r, sib)

    go(h0_copy())

    for h in range(ZH):
        for d in (0,) + order[:-1]:
            for s in range(2):
                if s or d:
                    e2_copy(h, s, d).wait_recv()
                    go(e3_copy(h, s, d, core))

    def h1_copy(d):
        return rc(halves.at[(y + d) % Y], h1_in.at[d], h1_s.at[d], h1_r.at[d], at_y(d))

    h0_copy().wait_recv()
    halves[...] = wg_out[pl.ds(core * Y, Y)] + h0_in[...]
    for d in range(1, Y):
        go(h1_copy(d))

    flush(2 * Y)
    for h in range(ZH):
        for s in range(2):
            for d in range(Y):
                e3_copy(h, s, d, 1 - core).wait_recv()

    zz = zh * ZL + z

    def h2_copy(i, to):
        h, d = (zh + i // ZL) % ZH, i % ZL
        v = (z + (d if to else ZL - d)) % ZL
        slot = h2_buf.at[zz] if to else h2_buf.at[h * ZL + v]
        dev = (x * ZL + v, rep_of(h, y, core))
        return rc(slot, slot, h2_s.at[i], h2_r.at[i], dev)

    unit = halves[y]
    for d in range(1, Y):
        h1_copy(d).wait_recv()
        unit = unit + h1_in[d]
    h2_buf[zz] = unit.astype(bf16)
    for i in range(1, ZH * ZL):
        go(h2_copy(i, True))

    def backward(n):
        out = None
        for s in range(2):
            q = s * SL + 2 * n
            lhs = jnp.concatenate(
                [slopes[table[6 + 2 * s, n]], slopes[table[7 + 2 * s, n]]], axis=1
            )
            term = dot(lhs, adj[pl.ds(q, 2)].reshape(2 * T, T))
            out = term if out is None else out + term
        out = out.astype(bf16)
        terms[n] = out

    def gx_copy(k, e):
        first = ((x + e) % X) * ZL + (ohalf, half)[k] * ZQ
        return rc(terms.at[pl.ds(first, ZQ)], gx_in.at[k, e], gx_s.at[k, e], gx_r.at[k, e], at_x(e))

    for k in range(2):
        for e in tuple(range(1, X)) + (0,):
            first = ((x + e) % X) * ZL + (ohalf, half)[k] * ZQ
            for i in range(ZQ):
                backward(first + i)
            if e:
                go(gx_copy(k, e))

    def gx_sum(k, v):
        t = terms[x * ZL + (ohalf, half)[k] * ZQ + v].astype(f32)
        for e in range(1, X):
            t = t + gx_in[k, e, v].astype(f32)
        return t

    def gz_copy(k, m):
        v = (zq + m) % ZQ
        return rc(
            gz_out.at[k, m],
            gz_in.at[k, m],
            gz_s.at[k, m],
            gz_r.at[k, m],
            (x * ZL + half * ZQ + v, r),
        )

    def gx_wait(k):
        for e in range(1, X):
            gx_copy(k, e).wait_recv()
        for m in range(1, ZQ):
            gz_out[k, m] = gx_sum(k, (zq + m) % ZQ).astype(bf16)
            go(gz_copy(k, m))
        return gx_sum(k, zq)

    crossing = gx_wait(0)

    def h3_copy(e, v):
        return rc(h3_buf.at[v], h3_buf.at[v], h3_s.at[e], h3_r.at[e], at_x(e))

    for i in range(1, ZH * ZL):
        h2_copy(i, False).wait_recv()
    unit = h2_buf[0].astype(f32)
    for i in range(1, ZH * ZL):
        unit = unit + h2_buf[i].astype(f32)
    h3_buf[x] = unit
    for e in range(1, X):
        go(h3_copy(e, x))

    kept = gx_wait(1)

    def h4_copy(d, v):
        slot = wg_all.at[core * Y + v]
        return rc(slot, slot, h4_s.at[d], h4_r.at[d], at_y(d))

    def h5_copy(d, c):
        slot = wg_all.at[c * Y + (y + Y - d) % Y]
        return rc(slot, slot, h5_s.at[d], h5_r.at[d], sib)

    for e in range(1, X):
        h3_copy(e, (x + X - e) % X).wait_recv()
    unit = h3_buf[0]
    for e in range(1, X):
        unit = unit + h3_buf[e]
    wg_all[core * Y + y] = unit
    for d in range(1, Y):
        go(h4_copy(d, y))
    go(h5_copy(0, core))

    def gz2_copy():
        return rc(gz2_out, gz2_in, gz2_s, gz2_r, (x * ZL + ohalf * ZQ + zq, r))

    for m in range(1, ZQ):
        gz_copy(0, m).wait_recv()
        crossing = crossing + gz_in[0, m].astype(f32)
    gz2_out[...] = crossing.astype(bf16)
    go(gz2_copy())
    for m in range(1, ZQ):
        gz_copy(1, m).wait_recv()
        kept = kept + gz_in[1, m].astype(f32)

    flush(1)
    for d in range(1, Y):
        h4_copy(d, (y + Y - d) % Y).wait_recv()
        go(h5_copy(d, core))

    for d in range(Y):
        h5_copy(d, 1 - core).wait_recv()
    weight_grad[...] = wg_all[...].reshape(T, T).T

    gz2_copy().wait_recv()
    pulled = (kept + gz2_in[...].astype(f32)).T.astype(bf16)
    input_grad[...] = lax.dot_general(
        pulled, w, (((1,), (1,)), ((), ())), preferred_element_type=f32
    ).astype(bf16)

    flush(0)


def local(features, weight, adjacency, row_tiles, live_counts, upstream):
    BLK, REP = X * ZL, ZH * Y * 2
    f32, bf16 = jnp.float32, jnp.bfloat16
    adj = adjacency.reshape(4 * BLK, T, T)
    rows = jnp.swapaxes(row_tiles, 3, 4).reshape(2, 2, BLK)
    live = live_counts.reshape(2, BLK)
    vmem = pl.BlockSpec(memory_space=pltpu.VMEM)

    def buf(*dims, dtype=bf16):
        return pltpu.VMEM(dims + (T,), dtype)

    U = T // (2 * Y)
    dma = pltpu.SemaphoreType.DMA
    scratch = [
        buf(4 * BLK, T),
        buf(T),
        buf(T),
        buf(T),
        pltpu.VMEM((2, 2, BLK), jnp.int32),
        pltpu.VMEM((2, BLK), jnp.int32),
        buf(16, dtype=jnp.int32),
        pltpu.SMEM((16, T), jnp.int32),
        buf(BLK, T),
        buf(4 * BLK + 1, T, dtype=f32),
        buf(ZH, Y, 2, T),
        buf(ZH, Y, 2, T),
        buf(ZH, 2, Y, T),
        buf(ZH, 2, Y, T),
        buf(ZH, T, dtype=f32),
        buf(ZH, T),
        buf(ZH, T),
        buf(ZH, T),
        buf(2 * REP + 1, T),
        buf(BLK, T),
        buf(2, X, ZQ, T),
        buf(2, ZQ, T),
        buf(2, ZQ, T),
        buf(T),
        buf(T),
        buf(2 * Y, U, dtype=f32),
        buf(Y, U, dtype=f32),
        buf(Y, U, dtype=f32),
        buf(Y, U, dtype=f32),
        buf(ZH * ZL, U),
        buf(X, U, dtype=f32),
        buf(2 * Y, U, dtype=f32),
        dma((7,)),
        dma((ZL,)),
        dma((ZL,)),
        dma((X, ZL)),
        dma((X, ZL)),
        dma,
        dma,
        dma((ZH, Y)),
        dma((ZH, Y)),
        dma((ZH, 2, Y)),
        dma((ZH, 2, Y)),
        dma((ZH,)),
        dma((ZH,)),
        dma((ZH, 2, Y)),
        dma((ZH, 2, Y)),
        dma((ZH, 2, Y)),
        dma((ZH, 2, Y)),
        dma((2, X)),
        dma((2, X)),
        dma((2, ZQ)),
        dma((2, ZQ)),
        dma,
        dma,
        dma,
        dma,
        dma((Y,)),
        dma((Y,)),
        dma((ZH * ZL,)),
        dma((ZH * ZL,)),
        dma((X,)),
        dma((X,)),
        dma((Y,)),
        dma((Y,)),
        dma((Y,)),
        dma((Y,)),
    ]
    return pl.pallas_call(
        kernel,
        name="graph_layer",
        out_shape=(
            jax.ShapeDtypeStruct((T, T), bf16),
            jax.ShapeDtypeStruct((T, T), bf16),
            jax.ShapeDtypeStruct((T, T), f32),
        ),
        in_specs=[pl.BlockSpec(memory_space=pltpu.HBM)] * 6,
        out_specs=(vmem, vmem, vmem),
        scratch_shapes=scratch,
        compiler_params=pltpu.CompilerParams(
            collective_id=0, has_side_effects=True, vmem_limit_bytes=48 * 1024 * 1024
        ),
    )(
        *(
            pltpu.with_memory_space_constraint(v, pltpu.HBM)
            for v in (features, weight, upstream, adj, rows, live)
        )
    )


def solution(mesh):
    assert mesh.shape["blk"] == X * ZL and mesh.shape["rep"] == ZH * Y * 2
    in_specs = (
        P(("blk", "rep"), None),
        P(),
        P("blk", "rep", None, None, None, None, None),
        P("blk", "rep", None, None, None),
        P("blk", "rep", None, None),
        P(("blk", "rep"), None),
    )
    out_specs = (P(("blk", "rep"), None), P(("blk", "rep"), None), P())
    return jax.shard_map(local, mesh=mesh, in_specs=in_specs, out_specs=out_specs, check_vma=False)
```

```python
import functools

import jax
import jax.numpy as jnp
from jax import lax
from jax.experimental import pallas as pl
from jax.experimental.pallas import tpu as pltpu
from jax.sharding import PartitionSpec as P

MESH = pl.DeviceIdType.MESH
X, ZL, ZH, Y = 4, 8, 2, 4
ZQ = ZL // 2
T = 128


def dot(a, b):
    return jnp.dot(a, b, preferred_element_type=jnp.float32)


def kernel(
    feat_hbm,
    weight_hbm,
    up_hbm,
    adj_hbm,
    rows_hbm,
    live_hbm,
    hidden,
    input_grad,
    weight_grad,
    adj,
    up,
    up_far,
    weight,
    rows_v,
    live_v,
    tab_v,
    table,
    feats,
    sums,
    c1_out,
    c1_in,
    c2_out,
    c2_in,
    part,
    c3_out,
    c3_in,
    tops,
    slopes,
    terms,
    gx_out,
    gx_in,
    gz_out,
    gz_in,
    gz2_out,
    gz2_in,
    wg_out,
    h0_in,
    halves,
    h1_in,
    h2_buf,
    h3_buf,
    wg_all,
    in_sem,
    az_s,
    az_r,
    ax_s,
    ax_r,
    up_s,
    up_r,
    c1_s,
    c1_r,
    c2_s,
    c2_r,
    c3_s,
    c3_r,
    e2_s,
    e2_r,
    e3_s,
    e3_r,
    gx_s,
    gx_r,
    gz_s,
    gz_r,
    gz2_s,
    gz2_r,
    h0_s,
    h0_r,
    h1_s,
    h1_r,
    h2_s,
    h2_r,
    h3_s,
    h3_r,
    h4_s,
    h4_r,
    h5_s,
    h5_r,
):
    BLK, REP = X * ZL, ZH * Y * 2
    SL = 2 * BLK
    f32, bf16 = jnp.float32, jnp.bfloat16
    b = lax.axis_index("blk")
    r = lax.axis_index("rep")
    x, z = b // ZL, b % ZL
    zh, y, core = r // (2 * Y), (r // 2) % Y, r % 2
    ozh = (zh + 1) % ZH
    b_up, b_dn = (b + 1) % BLK, (b + BLK - 1) % BLK

    def at_z(d):
        return (x * ZL + (z + d) % ZL, r)

    def at_x(d):
        return (((x + d) % X) * ZL + z, r)

    def rep_of(h, v, c):
        return (h * Y + v) * 2 + c

    def at_y(d):
        return (b, rep_of(zh, (y + d) % Y, core))

    first, last = (ZL - z) // ZL, (z + 1) // ZL

    def at_dn(d):
        return (b_dn, rep_of((zh + first) % ZH, (y + d) % Y, core))

    def at_up(d):
        return (b_up, rep_of((zh + last) % ZH, (y + d) % Y, core))

    sib = (b, rep_of(zh, y, 1 - core))
    r_oz = rep_of(ozh, y, core)

    def rc(src, dst, ss, rs, dev):
        return pltpu.make_async_remote_copy(
            src_ref=src, dst_ref=dst, send_sem=ss, recv_sem=rs, device_id=dev, device_id_type=MESH
        )

    in_copies = [
        pltpu.make_async_copy(src, dst, in_sem.at[i])
        for i, (src, dst) in enumerate(
            (
                (feat_hbm, feats.at[b]),
                (rows_hbm, rows_v),
                (live_hbm, live_v),
                (weight_hbm, weight),
                (adj_hbm, adj),
                (up_hbm, up),
            )
        )
    ]
    for copy in in_copies:
        copy.start()

    bar = pltpu.get_barrier_semaphore()

    def greet(dev):
        pl.semaphore_signal(bar, inc=1, device_id=dev, device_id_type=MESH)

    for i in reversed(range(1, ZH * ZL)):
        greet((x * ZL + (z + i % ZL) % ZL, rep_of((zh + i // ZL) % ZH, y, core)))
    for d in range(1, X):
        greet(at_x(d))
    for d in range(1, Y):
        greet(at_y(d))
    greet(sib)
    for d in range(Y):
        greet(at_up(d))
        greet(at_dn(d))

    half, zq = z // ZQ, z % ZQ
    ohalf = 1 - half

    sums[2 * SL] = jnp.zeros((T, T), f32)
    slopes[2 * REP] = jnp.zeros((T, T), bf16)
    in_copies[0].wait()

    sends = []

    def go(copy):
        copy.start()
        sends.append(copy)
        return copy

    def flush(keep):
        done = sends[: len(sends) - keep]
        del sends[: len(done)]
        for copy in done:
            copy.wait_send()

    pl.semaphore_wait(bar, (ZH * ZL - 1) + (X - 1) + (Y - 1) + 1 + 2 * Y)

    def zsrc(g):
        return (half, ohalf)[g // ZQ] * ZQ + (zq + ZQ - g % ZQ) % ZQ

    def mate(m):
        return (x * ZL + half * ZQ + (zq + m) % ZQ, r)

    partner = (x * ZL + ohalf * ZQ + zq, r)

    def az_copy(g, v, dev):
        slot = feats.at[x * ZL + v]
        return rc(slot, slot, az_s.at[g], az_r.at[g], dev)

    def ax_copy(g, e, v):
        slot = feats.at[v * ZL + zsrc(g)]
        return rc(slot, slot, ax_s.at[e, g], ax_r.at[e, g], at_x(e))

    def along_x(g):
        for e in range(1, X):
            go(ax_copy(g, e, x))

    go(az_copy(ZQ, z, partner))
    for m in range(1, ZQ):
        go(az_copy(m, z, mate(m)))
    along_x(0)

    in_copies[1].wait()
    in_copies[2].wait()
    i_s = lax.broadcasted_iota(jnp.int32, (BLK, BLK), 0)
    i_l = lax.broadcasted_iota(jnp.int32, (BLK, BLK), 1)

    def rank(n):
        far = ((n // ZQ) % 2) ^ half
        return (far * ZQ + ((zq - n % ZQ) & (ZQ - 1))) * X + ((x - n // ZL) & (X - 1))

    rank_s, rank_l = rank(i_s), rank(i_l)

    def to_rows(lanes):
        return jnp.sum(jnp.where(i_s == i_l, lanes, 0), axis=1, keepdims=True)

    t_l = lax.broadcasted_iota(jnp.int32, (BLK, REP), 1)
    for s in range(2):
        row_s = [to_rows(rows_v[s, k : k + 1, :]) for k in range(2)]
        live_l = live_v[s : s + 1, :]
        live_s = to_rows(live_l)
        code = [(2 * rank_s + k) * 1024 + s * SL + 2 * i_s + k for k in range(2)]

        def best(hits):
            found = jnp.max(jnp.maximum(hits[0], hits[1]), axis=0, keepdims=True)
            return jnp.where(found < 0, 2 * SL, found & 1023)

        for k in range(2):
            row_l = rows_v[s, k : k + 1, :]
            hits = [
                jnp.where(
                    (row_s[o] == row_l) & (live_s > o) & (2 * rank_s + o < 2 * rank_l + k),
                    code[o],
                    -1,
                )
                for o in range(2)
            ]
            tab_v[2 * s + k : 2 * s + k + 1, :BLK] = best(hits)
            spot = (((row_l & 1) * Y + ((row_l // 2) & (Y - 1))) * ZH + row_l // (2 * Y)) * 2 + s
            tab_v[6 + 2 * s + k : 7 + 2 * s + k, :BLK] = jnp.where(live_l > k, spot, 2 * REP)
        hits = [
            jnp.where((row_s[o] == t_l) & (live_s > o), code[o][:, :1], -1) for o in range(2)
        ]
        tab_v[4 + s : 5 + s, :REP] = best(hits)
    to_scalars = pltpu.make_async_copy(tab_v, table, in_sem.at[6])
    to_scalars.start()

    for m in range(1, ZQ):
        az_copy(m, zsrc(m), mate(m)).wait_recv()
        along_x(m)
    az_copy(ZQ, zsrc(ZQ), partner).wait_recv()
    for m in range(1, ZQ):
        go(az_copy(ZQ + m, zsrc(ZQ), mate(m)))
    along_x(ZQ)
    in_copies[4].wait()
    to_scalars.wait()


    def forward(g):
        for e in range(X):
            v = (x + X - e) % X
            if e:
                ax_copy(g, e, v).wait_recv()
            n = v * ZL + zsrc(g)
            for s in range(2):
                q = s * SL + 2 * n
                prod = dot(adj[pl.ds(q, 2)].reshape(2 * T, T), feats[n])
                sums[q] = prod[:T] + sums[table[2 * s, n]]
                sums[q + 1] = prod[T:] + sums[table[2 * s + 1, n]]

    early = ZQ - 1
    for g in range(early):
        forward(g)
    for m in range(1, ZQ):
        az_copy(ZQ + m, zsrc(ZQ + m), mate(m)).wait_recv()
        along_x(ZQ + m)
    for g in range(early, ZL):
        forward(g)

    def routed(s, t):
        return sums[table[4 + s, t]]

    def up_copy():
        return rc(up, up_far, up_s, up_r, (b, r_oz))

    in_copies[5].wait()
    go(up_copy())
    order = tuple(range(1, Y)) + (0,)

    def c1_copy(h, d):
        return rc(c1_out.at[h, d], c1_in.at[h, d], c1_s.at[h, d], c1_r.at[h, d], sib)

    def c2_copy(h, s, d):
        dev = at_dn(d) if s else at_y(d)
        i = (h, s, d)
        return rc(c2_out.at[i], c2_in.at[i], c2_s.at[i], c2_r.at[i], dev)

    def c3_copy(h):
        return rc(c3_out.at[h], c3_in.at[h], c3_s.at[h], c3_r.at[h], (b, r_oz))

    for h in range(ZH):
        for d in order:
            for s in range(2):
                c1_out[h, d, s] = routed(s, rep_of(h, (y + d) % Y, 1 - core)).astype(bf16)
            go(c1_copy(h, d))
    for h in range(ZH):
        for d in order:
            c1_copy(h, d).wait_recv()
            for s in (1, 0):
                both = routed(s, rep_of(h, (y + d) % Y, core)) + c1_in[h, d, s].astype(f32)
                if s or d:
                    c2_out[h, s, d] = both.astype(bf16)
                    go(c2_copy(h, s, d))
                else:
                    part[h] = both
    for h in range(ZH):
        t = part[h]
        for s in range(2):
            for d in range(1 - s, Y):
                c2_copy(h, s, d).wait_recv()
                t = t + c2_in[h, s, d].astype(f32)
        part[h] = t
        c3_out[h] = t.astype(bf16)
        go(c3_copy(h))
    flush(ZH)
    up_copy().wait_recv()

    def place(s, h, v, c):
        return ((c * Y + v) * ZH + h) * 2 + s

    def tile(s, h, v, c):
        return slopes.at[place(s, h, v, c)]

    def e2_copy(h, s, d):
        dev = at_up(d) if s else at_y(d)
        own = tile(0, h, y, core)
        return rc(own, tile(s, h, y, core), e2_s.at[h, s, d], e2_r.at[h, s, d], dev)

    def e3_copy(h, d, c):
        both = slopes.at[pl.ds(place(0, h, (y + Y - d) % Y, c), 2)]
        return rc(both, both, e3_s.at[h, d], e3_r.at[h, d], sib)

    in_copies[3].wait()
    w = weight[...]
    for h in range(ZH):
        c3_copy(h).wait_recv()
        gathered = part[h] + c3_in[h].astype(f32)
        high = gathered.astype(bf16)
        low = (gathered - high.astype(f32)).astype(bf16)
        tops[h] = high
        summed = dot(high, w) + dot(low, w)
        sig = jax.nn.sigmoid(summed)
        given = jnp.where(zh == h, up[...], up_far[...]).astype(f32)
        slope = given * (sig * (1.0 + summed * (1.0 - sig)))
        slopes[place(0, h, y, core)] = slope.T.astype(bf16)
        for d in order:
            go(e2_copy(h, 1, d))
            if d:
                go(e2_copy(h, 0, d))
        part[h] = summed * sig
    hidden[...] = part[zh].astype(bf16)

    U = T // (2 * Y)
    total = dot(slopes[place(0, zh, y, core)], tops[zh])
    wg_out[...] = total.reshape(2 * Y, U, T)

    def h0_copy():
        return rc(wg_out.at[pl.ds((1 - core) * Y, Y)], h0_in, h0_s, h0_r, sib)

    go(h0_copy())

    def h1_copy(d):
        return rc(halves.at[(y + d) % Y], h1_in.at[d], h1_s.at[d], h1_r.at[d], at_y(d))

    h0_copy().wait_recv()
    halves[...] = wg_out[pl.ds(core * Y, Y)] + h0_in[...]
    for d in range(1, Y):
        go(h1_copy(d))

    def to_sibling(h):
        for d in (0,) + order[:-1]:
            for s in range(2):
                if s or d:
                    e2_copy(h, s, d).wait_recv()
            go(e3_copy(h, d, core))

    to_sibling(0)

    zz = zh * ZL + z

    def h2_copy(i, to):
        h, d = (zh + i // ZL) % ZH, i % ZL
        v = (z + (d if to else ZL - d)) % ZL
        slot = h2_buf.at[zz] if to else h2_buf.at[h * ZL + v]
        dev = (x * ZL + v, rep_of(h, y, core))
        return rc(slot, slot, h2_s.at[i], h2_r.at[i], dev)

    unit = halves[y]
    for d in range(1, Y):
        h1_copy(d).wait_recv()
        unit = unit + h1_in[d]
    h2_buf[zz] = unit.astype(bf16)
    for i in range(1, ZH * ZL):
        go(h2_copy(i, True))

    for h in range(1, ZH):
        to_sibling(h)

    flush(Y)
    for h in range(ZH):
        for d in range(Y):
            e3_copy(h, d, 1 - core).wait_recv()

    def backward(n):
        out = None
        for s in range(2):
            q = s * SL + 2 * n
            lhs = jnp.concatenate(
                [slopes[table[6 + 2 * s, n]], slopes[table[7 + 2 * s, n]]], axis=1
            )
            term = dot(lhs, adj[pl.ds(q, 2)].reshape(2 * T, T))
            out = term if out is None else out + term
        out = out.astype(bf16)
        terms[n] = out

    ZP = ZQ // 2
    turn_x, mirror_x = x + 1 - 2 * (x % 2), X - 1 - x
    over_x = (x + X // 2) % X
    meets = ((turn_x, mirror_x), (mirror_x, turn_x))

    def spot_of(v, k, g):
        return v * ZL + (ohalf, half)[k] * ZQ + g * ZP

    def gx_copy(k, g, step):
        to = (meets[g][step // 2] * ZL + z, r)
        i = (k, g, step)
        if step == 2:
            src = gx_out.at[k, g]
        else:
            src = terms.at[pl.ds(spot_of((over_x, meets[g][0])[step], k, g), ZP)]
        return rc(src, gx_in.at[i], gx_s.at[i], gx_r.at[i], to)

    def column_tiles(v, k):
        for g in range(2):
            for i in range(ZP):
                backward(spot_of(v[g], k, g) + i)

    def first_step(k, step):
        column_tiles(((over_x, over_x), (turn_x, mirror_x))[step], k)
        for g in range(2):
            go(gx_copy(k, g, step))

    def second_step(k):
        for g in range(2):
            gx_copy(k, g, 0).wait_recv()
            mine = terms[pl.ds(spot_of(meets[g][1], k, g), ZP)].astype(f32)
            gx_out[k, g] = (mine + gx_in[k, g, 0].astype(f32)).astype(bf16)
            go(gx_copy(k, g, 2))

    first_step(0, 0)
    first_step(0, 1)
    first_step(1, 0)
    for k in range(2):
        column_tiles((mirror_x, turn_x), k)
    second_step(0)
    first_step(1, 1)
    for k in range(2):
        column_tiles((x, x), k)
    second_step(1)

    def gx_sum(k, v):
        g, i = v // ZP, v % ZP
        t = terms[spot_of(x, k, 0) + v].astype(f32)
        return t + gx_in[k, g, 1, i].astype(f32) + gx_in[k, g, 2, i].astype(f32)

    def gz_copy(k, m):
        v = (zq + m) % ZQ
        return rc(
            gz_out.at[k, m],
            gz_in.at[k, m],
            gz_s.at[k, m],
            gz_r.at[k, m],
            (x * ZL + half * ZQ + v, r),
        )

    def gx_wait(k):
        for g in range(2):
            for step in (1, 2):
                gx_copy(k, g, step).wait_recv()
        for m in range(1, ZQ):
            gz_out[k, m] = gx_sum(k, (zq + m) % ZQ).astype(bf16)
            go(gz_copy(k, m))
        return gx_sum(k, zq)

    crossing = gx_wait(0)

    def h3_copy(e, v):
        return rc(h3_buf.at[v], h3_buf.at[v], h3_s.at[e], h3_r.at[e], at_x(e))

    for i in range(1, ZH * ZL):
        h2_copy(i, False).wait_recv()
    unit = h2_buf[0].astype(f32)
    for i in range(1, ZH * ZL):
        unit = unit + h2_buf[i].astype(f32)
    h3_buf[x] = unit
    for e in range(1, X):
        go(h3_copy(e, x))

    kept = gx_wait(1)

    def h4_copy(d, v):
        slot = wg_all.at[core * Y + v]
        return rc(slot, slot, h4_s.at[d], h4_r.at[d], at_y(d))

    def h5_copy(d, c):
        slot = wg_all.at[c * Y + (y + Y - d) % Y]
        return rc(slot, slot, h5_s.at[d], h5_r.at[d], sib)

    for e in range(1, X):
        h3_copy(e, (x + X - e) % X).wait_recv()
    unit = h3_buf[0]
    for e in range(1, X):
        unit = unit + h3_buf[e]
    wg_all[core * Y + y] = unit
    for d in range(1, Y):
        go(h4_copy(d, y))
    go(h5_copy(0, core))

    def gz2_copy():
        return rc(gz2_out, gz2_in, gz2_s, gz2_r, (x * ZL + ohalf * ZQ + zq, r))

    for m in range(1, ZQ):
        gz_copy(0, m).wait_recv()
        crossing = crossing + gz_in[0, m].astype(f32)
    gz2_out[...] = crossing.astype(bf16)
    go(gz2_copy())
    for m in range(1, ZQ):
        gz_copy(1, m).wait_recv()
        kept = kept + gz_in[1, m].astype(f32)

    flush(1)
    for d in range(1, Y):
        h4_copy(d, (y + Y - d) % Y).wait_recv()
        go(h5_copy(d, core))

    for d in range(Y):
        h5_copy(d, 1 - core).wait_recv()
    weight_grad[...] = wg_all[...].reshape(T, T).T

    gz2_copy().wait_recv()
    pulled = (kept + gz2_in[...].astype(f32)).T.astype(bf16)
    input_grad[...] = lax.dot_general(
        pulled, w, (((1,), (1,)), ((), ())), preferred_element_type=f32
    ).astype(bf16)

    flush(0)


def local(features, weight, adjacency, row_tiles, live_counts, upstream):
    BLK, REP = X * ZL, ZH * Y * 2
    f32, bf16 = jnp.float32, jnp.bfloat16
    adj = adjacency.reshape(4 * BLK, T, T)
    rows = jnp.swapaxes(row_tiles, 3, 4).reshape(2, 2, BLK)
    live = live_counts.reshape(2, BLK)
    vmem = pl.BlockSpec(memory_space=pltpu.VMEM)

    def buf(*dims, dtype=bf16):
        return pltpu.VMEM(dims + (T,), dtype)

    U = T // (2 * Y)
    dma = pltpu.SemaphoreType.DMA
    scratch = [
        buf(4 * BLK, T),
        buf(T),
        buf(T),
        buf(T),
        pltpu.VMEM((2, 2, BLK), jnp.int32),
        pltpu.VMEM((2, BLK), jnp.int32),
        buf(16, dtype=jnp.int32),
        pltpu.SMEM((16, T), jnp.int32),
        buf(BLK, T),
        buf(4 * BLK + 1, T, dtype=f32),
        buf(ZH, Y, 2, T),
        buf(ZH, Y, 2, T),
        buf(ZH, 2, Y, T),
        buf(ZH, 2, Y, T),
        buf(ZH, T, dtype=f32),
        buf(ZH, T),
        buf(ZH, T),
        buf(ZH, T),
        buf(2 * REP + 1, T),
        buf(BLK, T),
        buf(2, 2, ZQ // 2, T),
        buf(2, 2, 3, ZQ // 2, T),
        buf(2, ZQ, T),
        buf(2, ZQ, T),
        buf(T),
        buf(T),
        buf(2 * Y, U, dtype=f32),
        buf(Y, U, dtype=f32),
        buf(Y, U, dtype=f32),
        buf(Y, U, dtype=f32),
        buf(ZH * ZL, U),
        buf(X, U, dtype=f32),
        buf(2 * Y, U, dtype=f32),
        dma((7,)),
        dma((ZL,)),
        dma((ZL,)),
        dma((X, ZL)),
        dma((X, ZL)),
        dma,
        dma,
        dma((ZH, Y)),
        dma((ZH, Y)),
        dma((ZH, 2, Y)),
        dma((ZH, 2, Y)),
        dma((ZH,)),
        dma((ZH,)),
        dma((ZH, 2, Y)),
        dma((ZH, 2, Y)),
        dma((ZH, Y)),
        dma((ZH, Y)),
        dma((2, 2, 3)),
        dma((2, 2, 3)),
        dma((2, ZQ)),
        dma((2, ZQ)),
        dma,
        dma,
        dma,
        dma,
        dma((Y,)),
        dma((Y,)),
        dma((ZH * ZL,)),
        dma((ZH * ZL,)),
        dma((X,)),
        dma((X,)),
        dma((Y,)),
        dma((Y,)),
        dma((Y,)),
        dma((Y,)),
    ]
    return pl.pallas_call(
        kernel,
        name="graph_layer",
        out_shape=(
            jax.ShapeDtypeStruct((T, T), bf16),
            jax.ShapeDtypeStruct((T, T), bf16),
            jax.ShapeDtypeStruct((T, T), f32),
        ),
        in_specs=[pl.BlockSpec(memory_space=pltpu.HBM)] * 6,
        out_specs=(vmem, vmem, vmem),
        scratch_shapes=scratch,
        compiler_params=pltpu.CompilerParams(
            collective_id=0, has_side_effects=True, vmem_limit_bytes=48 * 1024 * 1024
        ),
    )(
        *(
            pltpu.with_memory_space_constraint(v, pltpu.HBM)
            for v in (features, weight, upstream, adj, rows, live)
        )
    )


def solution(mesh):
    assert mesh.shape["blk"] == X * ZL and mesh.shape["rep"] == ZH * Y * 2
    in_specs = (
        P(("blk", "rep"), None),
        P(),
        P("blk", "rep", None, None, None, None, None),
        P("blk", "rep", None, None, None),
        P("blk", "rep", None, None),
        P(("blk", "rep"), None),
    )
    out_specs = (P(("blk", "rep"), None), P(("blk", "rep"), None), P())
    return jax.shard_map(local, mesh=mesh, in_specs=in_specs, out_specs=out_specs, check_vma=False)
```

```python
import functools

import jax
import jax.numpy as jnp
from jax import lax
from jax.experimental import pallas as pl
from jax.experimental.pallas import tpu as pltpu
from jax.sharding import PartitionSpec as P

MESH = pl.DeviceIdType.MESH
X, ZL, ZH, Y = 4, 8, 2, 4
ZQ = ZL // 2
T = 128


def dot(a, b):
    return jnp.dot(a, b, preferred_element_type=jnp.float32)


def kernel(
    feat_hbm,
    weight_hbm,
    up_hbm,
    adj_hbm,
    rows_hbm,
    live_hbm,
    hidden,
    input_grad,
    weight_grad,
    adj,
    up,
    up_far,
    weight,
    rows_v,
    live_v,
    tab_v,
    table,
    feats,
    sums,
    c1_out,
    c1_in,
    c2_out,
    c2_in,
    part,
    c3_out,
    c3_in,
    tops,
    slopes,
    terms,
    gx_out,
    gx_in,
    gz_out,
    gz_in,
    gz2_out,
    gz2_in,
    wg_out,
    h0_in,
    halves,
    h1_in,
    h2_buf,
    h3_buf,
    wg_all,
    ring_sem,
    in_sem,
    az_s,
    az_r,
    ax_s,
    ax_r,
    up_s,
    up_r,
    c1_s,
    c1_r,
    c2_s,
    c2_r,
    c3_s,
    c3_r,
    e2_s,
    e2_r,
    e3_s,
    e3_r,
    gx_s,
    gx_r,
    gz_s,
    gz_r,
    gz2_s,
    gz2_r,
    h0_s,
    h0_r,
    h1_s,
    h1_r,
    h2_s,
    h2_r,
    h3_s,
    h3_r,
    h4_s,
    h4_r,
    h5_s,
    h5_r,
):
    BLK, REP = X * ZL, ZH * Y * 2
    SL = 2 * BLK
    f32, bf16 = jnp.float32, jnp.bfloat16
    b = lax.axis_index("blk")
    r = lax.axis_index("rep")
    x, z = b // ZL, b % ZL
    zh, y, core = r // (2 * Y), (r // 2) % Y, r % 2
    ozh = (zh + 1) % ZH
    b_up, b_dn = (b + 1) % BLK, (b + BLK - 1) % BLK

    def at_z(d):
        return (x * ZL + (z + d) % ZL, r)

    def at_x(d):
        return (((x + d) % X) * ZL + z, r)

    def rep_of(h, v, c):
        return (h * Y + v) * 2 + c

    def at_y(d):
        return (b, rep_of(zh, (y + d) % Y, core))

    first, last = (ZL - z) // ZL, (z + 1) // ZL

    def at_dn(d):
        return (b_dn, rep_of((zh + first) % ZH, (y + d) % Y, core))

    def at_up(d):
        return (b_up, rep_of((zh + last) % ZH, (y + d) % Y, core))

    def at_ring(i):
        v = (zh * ZL + z + i) % (ZH * ZL)
        return (x * ZL + v % ZL, rep_of(v // ZL, y, core))

    sib = (b, rep_of(zh, y, 1 - core))
    r_oz = rep_of(ozh, y, core)

    def rc(src, dst, ss, rs, dev):
        return pltpu.make_async_remote_copy(
            src_ref=src, dst_ref=dst, send_sem=ss, recv_sem=rs, device_id=dev, device_id_type=MESH
        )

    in_copies = [
        pltpu.make_async_copy(src, dst, in_sem.at[i])
        for i, (src, dst) in enumerate(
            (
                (feat_hbm, feats.at[b]),
                (rows_hbm, rows_v),
                (live_hbm, live_v),
                (weight_hbm, weight),
                (adj_hbm, adj),
                (up_hbm, up),
            )
        )
    ]
    for copy in in_copies:
        copy.start()

    bar = pltpu.get_barrier_semaphore()

    def greet(dev):
        pl.semaphore_signal(bar, inc=1, device_id=dev, device_id_type=MESH)

    for i in range(ZQ, 0, -1):
        greet(at_ring(i))
        greet(at_ring(ZH * ZL - i))
    for d in range(1, X):
        greet(at_x(d))
    for d in range(1, Y):
        greet(at_y(d))
    greet(sib)
    for d in range(Y):
        greet(at_up(d))
        greet(at_dn(d))

    half, zq = z // ZQ, z % ZQ
    ohalf = 1 - half

    sums[2 * SL] = jnp.zeros((T, T), f32)
    slopes[2 * REP] = jnp.zeros((T, T), bf16)
    in_copies[0].wait()

    sends = []

    def go(copy):
        copy.start()
        sends.append(copy)
        return copy

    def flush(keep):
        done = sends[: len(sends) - keep]
        del sends[: len(done)]
        for copy in done:
            copy.wait_send()

    pl.semaphore_wait(bar, 2 * ZQ + (X - 1) + (Y - 1) + 1 + 2 * Y)

    def zsrc(g):
        return (half, ohalf)[g // ZQ] * ZQ + (zq + ZQ - g % ZQ) % ZQ

    def mate(m):
        return (x * ZL + half * ZQ + (zq + m) % ZQ, r)

    partner = (x * ZL + ohalf * ZQ + zq, r)

    def az_copy(g, v, dev):
        slot = feats.at[x * ZL + v]
        return rc(slot, slot, az_s.at[g], az_r.at[g], dev)

    def ax_copy(g, e, v):
        slot = feats.at[v * ZL + zsrc(g)]
        return rc(slot, slot, ax_s.at[e, g], ax_r.at[e, g], at_x(e))

    def along_x(g):
        for e in range(1, X):
            go(ax_copy(g, e, x))

    go(az_copy(ZQ, z, partner))
    for m in range(1, ZQ):
        go(az_copy(m, z, mate(m)))
    along_x(0)

    for i in (ZQ, ZH * ZL - ZQ):
        pl.semaphore_signal(ring_sem, inc=1, device_id=at_ring(i), device_id_type=MESH)

    in_copies[1].wait()
    in_copies[2].wait()
    i_s = lax.broadcasted_iota(jnp.int32, (BLK, BLK), 0)
    i_l = lax.broadcasted_iota(jnp.int32, (BLK, BLK), 1)

    def rank(n):
        far = ((n // ZQ) % 2) ^ half
        return (far * ZQ + ((zq - n % ZQ) & (ZQ - 1))) * X + ((x - n // ZL) & (X - 1))

    rank_s, rank_l = rank(i_s), rank(i_l)

    def to_rows(lanes):
        return jnp.sum(jnp.where(i_s == i_l, lanes, 0), axis=1, keepdims=True)

    t_l = lax.broadcasted_iota(jnp.int32, (BLK, REP), 1)
    for s in range(2):
        row_s = [to_rows(rows_v[s, k : k + 1, :]) for k in range(2)]
        live_l = live_v[s : s + 1, :]
        live_s = to_rows(live_l)
        code = [(2 * rank_s + k) * 1024 + s * SL + 2 * i_s + k for k in range(2)]

        def best(hits):
            found = jnp.max(jnp.maximum(hits[0], hits[1]), axis=0, keepdims=True)
            return jnp.where(found < 0, 2 * SL, found & 1023)

        for k in range(2):
            row_l = rows_v[s, k : k + 1, :]
            hits = [
                jnp.where(
                    (row_s[o] == row_l) & (live_s > o) & (2 * rank_s + o < 2 * rank_l + k),
                    code[o],
                    -1,
                )
                for o in range(2)
            ]
            tab_v[2 * s + k : 2 * s + k + 1, :BLK] = best(hits)
            spot = (((row_l & 1) * Y + ((row_l // 2) & (Y - 1))) * ZH + row_l // (2 * Y)) * 2 + s
            tab_v[6 + 2 * s + k : 7 + 2 * s + k, :BLK] = jnp.where(live_l > k, spot, 2 * REP)
        hits = [
            jnp.where((row_s[o] == t_l) & (live_s > o), code[o][:, :1], -1) for o in range(2)
        ]
        tab_v[4 + s : 5 + s, :REP] = best(hits)
    to_scalars = pltpu.make_async_copy(tab_v, table, in_sem.at[6])
    to_scalars.start()

    for m in range(1, ZQ):
        az_copy(m, zsrc(m), mate(m)).wait_recv()
        along_x(m)
    az_copy(ZQ, zsrc(ZQ), partner).wait_recv()
    for m in range(1, ZQ):
        go(az_copy(ZQ + m, zsrc(ZQ), mate(m)))
    along_x(ZQ)
    in_copies[4].wait()
    to_scalars.wait()


    def forward(g):
        for e in range(X):
            v = (x + X - e) % X
            if e:
                ax_copy(g, e, v).wait_recv()
            n = v * ZL + zsrc(g)
            for s in range(2):
                q = s * SL + 2 * n
                prod = dot(adj[pl.ds(q, 2)].reshape(2 * T, T), feats[n])
                sums[q] = prod[:T] + sums[table[2 * s, n]]
                sums[q + 1] = prod[T:] + sums[table[2 * s + 1, n]]

    early = ZQ // 2
    for g in range(early):
        forward(g)
    for m in range(1, ZQ):
        az_copy(ZQ + m, zsrc(ZQ + m), mate(m)).wait_recv()
        along_x(ZQ + m)
    for g in range(early, ZL):
        forward(g)

    def routed(s, t):
        return sums[table[4 + s, t]]

    def up_copy():
        return rc(up, up_far, up_s, up_r, (b, r_oz))

    in_copies[5].wait()
    pl.semaphore_wait(ring_sem, 2)
    go(up_copy())
    order = tuple(sorted(range(1, Y), key=lambda d: -min(d, Y - d))) + (0,)

    def c1_copy(h, d):
        return rc(c1_out.at[h, d], c1_in.at[h, d], c1_s.at[h, d], c1_r.at[h, d], sib)

    def c2_copy(h, s, d):
        dev = at_dn(d) if s else at_y(d)
        i = (h, s, d)
        return rc(c2_out.at[i], c2_in.at[i], c2_s.at[i], c2_r.at[i], dev)

    def c3_copy(h):
        return rc(c3_out.at[h], c3_in.at[h], c3_s.at[h], c3_r.at[h], (b, r_oz))

    for h in range(ZH):
        for d in order:
            for s in range(2):
                c1_out[h, d, s] = routed(s, rep_of(h, (y + d) % Y, 1 - core)).astype(bf16)
            go(c1_copy(h, d))
    for h in range(ZH):
        for d in order:
            c1_copy(h, d).wait_recv()
            for s in (1, 0):
                both = routed(s, rep_of(h, (y + d) % Y, core)) + c1_in[h, d, s].astype(f32)
                if s or d:
                    c2_out[h, s, d] = both.astype(bf16)
                    go(c2_copy(h, s, d))
                else:
                    part[h] = both
    for h in range(ZH):
        t = part[h]
        for s in range(2):
            for d in range(1 - s, Y):
                c2_copy(h, s, d).wait_recv()
                t = t + c2_in[h, s, d].astype(f32)
        part[h] = t
        c3_out[h] = t.astype(bf16)
        go(c3_copy(h))
    flush(ZH)
    up_copy().wait_recv()

    def place(s, h, v, c):
        return ((c * Y + v) * ZH + h) * 2 + s

    def tile(s, h, v, c):
        return slopes.at[place(s, h, v, c)]

    def e2_copy(h, s, d):
        dev = at_up(d) if s else at_y(d)
        own = tile(0, h, y, core)
        return rc(own, tile(s, h, y, core), e2_s.at[h, s, d], e2_r.at[h, s, d], dev)

    def e3_copy(h, d, c):
        both = slopes.at[pl.ds(place(0, h, (y + Y - d) % Y, c), 2)]
        return rc(both, both, e3_s.at[h, d], e3_r.at[h, d], sib)

    in_copies[3].wait()
    w = weight[...]
    for h in range(ZH):
        c3_copy(h).wait_recv()
        gathered = part[h] + c3_in[h].astype(f32)
        high = gathered.astype(bf16)
        low = (gathered - high.astype(f32)).astype(bf16)
        tops[h] = high
        summed = dot(high, w) + dot(low, w)
        sig = jax.nn.sigmoid(summed)
        given = jnp.where(zh == h, up[...], up_far[...]).astype(f32)
        slope = given * (sig * (1.0 + summed * (1.0 - sig)))
        slopes[place(0, h, y, core)] = slope.T.astype(bf16)
        for d in order:
            go(e2_copy(h, 1, d))
            if d:
                go(e2_copy(h, 0, d))
        part[h] = summed * sig
    hidden[...] = part[zh].astype(bf16)

    U = T // (2 * Y)
    total = dot(slopes[place(0, zh, y, core)], tops[zh])
    wg_out[...] = total.reshape(2 * Y, U, T)

    def h0_copy():
        return rc(wg_out.at[pl.ds((1 - core) * Y, Y)], h0_in, h0_s, h0_r, sib)

    go(h0_copy())

    def h1_copy(d):
        return rc(halves.at[(y + d) % Y], h1_in.at[d], h1_s.at[d], h1_r.at[d], at_y(d))

    h0_copy().wait_recv()
    halves[...] = wg_out[pl.ds(core * Y, Y)] + h0_in[...]
    for d in range(1, Y):
        go(h1_copy(d))

    def to_sibling(h):
        for d in (0,) + order[:-1]:
            for s in range(2):
                if s or d:
                    e2_copy(h, s, d).wait_recv()
            go(e3_copy(h, d, core))

    to_sibling(0)

    zz = zh * ZL + z

    def h2_copy(i, to):
        h, d = (zh + i // ZL) % ZH, i % ZL
        v = (z + (d if to else ZL - d)) % ZL
        slot = h2_buf.at[zz] if to else h2_buf.at[h * ZL + v]
        dev = (x * ZL + v, rep_of(h, y, core))
        return rc(slot, slot, h2_s.at[i], h2_r.at[i], dev)

    unit = halves[y]
    for d in range(1, Y):
        h1_copy(d).wait_recv()
        unit = unit + h1_in[d]
    h2_buf[zz] = unit.astype(bf16)
    for i in range(1, ZH * ZL):
        go(h2_copy(i, True))

    for h in range(1, ZH):
        to_sibling(h)

    for h in range(ZH):
        for d in range(Y):
            e3_copy(h, d, 1 - core).wait_recv()

    def backward(n):
        out = None
        for s in range(2):
            q = s * SL + 2 * n
            lhs = jnp.concatenate(
                [slopes[table[6 + 2 * s, n]], slopes[table[7 + 2 * s, n]]], axis=1
            )
            term = dot(lhs, adj[pl.ds(q, 2)].reshape(2 * T, T))
            out = term if out is None else out + term
        out = out.astype(bf16)
        terms[n] = out

    ZP = ZQ // 2
    turn_x, mirror_x = x + 1 - 2 * (x % 2), X - 1 - x
    over_x = (x + X // 2) % X
    meets = ((turn_x, mirror_x), (mirror_x, turn_x))

    def spot_of(v, k, g):
        return v * ZL + (ohalf, half)[k] * ZQ + g * ZP

    def gx_copy(k, g, step):
        to = (meets[g][step // 2] * ZL + z, r)
        i = (k, g, step)
        if step == 2:
            src = gx_out.at[k, g]
        else:
            src = terms.at[pl.ds(spot_of((over_x, meets[g][0])[step], k, g), ZP)]
        return rc(src, gx_in.at[i], gx_s.at[i], gx_r.at[i], to)

    def column_tiles(v, k):
        for g in range(2):
            for i in range(ZP):
                backward(spot_of(v[g], k, g) + i)

    def first_step(k, step):
        column_tiles(((over_x, over_x), (turn_x, mirror_x))[step], k)
        for g in range(2):
            go(gx_copy(k, g, step))

    def second_step(k):
        for g in range(2):
            gx_copy(k, g, 0).wait_recv()
            mine = terms[pl.ds(spot_of(meets[g][1], k, g), ZP)].astype(f32)
            gx_out[k, g] = (mine + gx_in[k, g, 0].astype(f32)).astype(bf16)
            go(gx_copy(k, g, 2))

    first_step(0, 0)
    first_step(0, 1)
    first_step(1, 0)
    for k in range(2):
        column_tiles((mirror_x, turn_x), k)
    second_step(0)
    first_step(1, 1)
    for k in range(2):
        column_tiles((x, x), k)
    second_step(1)

    def gx_sum(k, v):
        g, i = v // ZP, v % ZP
        t = terms[spot_of(x, k, 0) + v].astype(f32)
        return t + gx_in[k, g, 1, i].astype(f32) + gx_in[k, g, 2, i].astype(f32)

    def gz_copy(k, m):
        v = (zq + m) % ZQ
        return rc(
            gz_out.at[k, m],
            gz_in.at[k, m],
            gz_s.at[k, m],
            gz_r.at[k, m],
            (x * ZL + half * ZQ + v, r),
        )

    def gx_wait(k):
        for g in range(2):
            for step in (1, 2):
                gx_copy(k, g, step).wait_recv()
        for m in range(1, ZQ):
            gz_out[k, m] = gx_sum(k, (zq + m) % ZQ).astype(bf16)
            go(gz_copy(k, m))
        return gx_sum(k, zq)

    flush(12)
    crossing = gx_wait(0)

    def h3_copy(e, v):
        return rc(h3_buf.at[v], h3_buf.at[v], h3_s.at[e], h3_r.at[e], at_x(e))

    for i in range(1, ZH * ZL):
        h2_copy(i, False).wait_recv()
    unit = h2_buf[0].astype(f32)
    for i in range(1, ZH * ZL):
        unit = unit + h2_buf[i].astype(f32)
    h3_buf[x] = unit
    for e in range(1, X):
        go(h3_copy(e, x))

    kept = gx_wait(1)

    def h4_copy(d, v):
        slot = wg_all.at[core * Y + v]
        return rc(slot, slot, h4_s.at[d], h4_r.at[d], at_y(d))

    def h5_copy(d, c):
        slot = wg_all.at[c * Y + (y + Y - d) % Y]
        return rc(slot, slot, h5_s.at[d], h5_r.at[d], sib)

    for e in range(1, X):
        h3_copy(e, (x + X - e) % X).wait_recv()
    unit = h3_buf[0]
    for e in range(1, X):
        unit = unit + h3_buf[e]
    wg_all[core * Y + y] = unit
    for d in range(1, Y):
        go(h4_copy(d, y))
    go(h5_copy(0, core))

    def gz2_copy():
        return rc(gz2_out, gz2_in, gz2_s, gz2_r, (x * ZL + ohalf * ZQ + zq, r))

    for m in range(1, ZQ):
        gz_copy(0, m).wait_recv()
        crossing = crossing + gz_in[0, m].astype(f32)
    gz2_out[...] = crossing.astype(bf16)
    go(gz2_copy())
    for m in range(1, ZQ):
        gz_copy(1, m).wait_recv()
        kept = kept + gz_in[1, m].astype(f32)

    flush(1)
    for d in range(1, Y):
        h4_copy(d, (y + Y - d) % Y).wait_recv()
        go(h5_copy(d, core))

    for d in range(Y):
        h5_copy(d, 1 - core).wait_recv()
    weight_grad[...] = wg_all[...].reshape(T, T).T

    gz2_copy().wait_recv()
    pulled = (kept + gz2_in[...].astype(f32)).T.astype(bf16)
    input_grad[...] = lax.dot_general(
        pulled, w, (((1,), (1,)), ((), ())), preferred_element_type=f32
    ).astype(bf16)

    flush(0)


def local(features, weight, adjacency, row_tiles, live_counts, upstream):
    BLK, REP = X * ZL, ZH * Y * 2
    f32, bf16 = jnp.float32, jnp.bfloat16
    adj = adjacency.reshape(4 * BLK, T, T)
    rows = jnp.swapaxes(row_tiles, 3, 4).reshape(2, 2, BLK)
    live = live_counts.reshape(2, BLK)
    vmem = pl.BlockSpec(memory_space=pltpu.VMEM)

    def buf(*dims, dtype=bf16):
        return pltpu.VMEM(dims + (T,), dtype)

    U = T // (2 * Y)
    dma = pltpu.SemaphoreType.DMA
    scratch = [
        buf(4 * BLK, T),
        buf(T),
        buf(T),
        buf(T),
        pltpu.VMEM((2, 2, BLK), jnp.int32),
        pltpu.VMEM((2, BLK), jnp.int32),
        buf(16, dtype=jnp.int32),
        pltpu.SMEM((16, T), jnp.int32),
        buf(BLK, T),
        buf(4 * BLK + 1, T, dtype=f32),
        buf(ZH, Y, 2, T),
        buf(ZH, Y, 2, T),
        buf(ZH, 2, Y, T),
        buf(ZH, 2, Y, T),
        buf(ZH, T, dtype=f32),
        buf(ZH, T),
        buf(ZH, T),
        buf(ZH, T),
        buf(2 * REP + 1, T),
        buf(BLK, T),
        buf(2, 2, ZQ // 2, T),
        buf(2, 2, 3, ZQ // 2, T),
        buf(2, ZQ, T),
        buf(2, ZQ, T),
        buf(T),
        buf(T),
        buf(2 * Y, U, dtype=f32),
        buf(Y, U, dtype=f32),
        buf(Y, U, dtype=f32),
        buf(Y, U, dtype=f32),
        buf(ZH * ZL, U),
        buf(X, U, dtype=f32),
        buf(2 * Y, U, dtype=f32),
        pltpu.SemaphoreType.REGULAR,
        dma((7,)),
        dma((ZL,)),
        dma((ZL,)),
        dma((X, ZL)),
        dma((X, ZL)),
        dma,
        dma,
        dma((ZH, Y)),
        dma((ZH, Y)),
        dma((ZH, 2, Y)),
        dma((ZH, 2, Y)),
        dma((ZH,)),
        dma((ZH,)),
        dma((ZH, 2, Y)),
        dma((ZH, 2, Y)),
        dma((ZH, Y)),
        dma((ZH, Y)),
        dma((2, 2, 3)),
        dma((2, 2, 3)),
        dma((2, ZQ)),
        dma((2, ZQ)),
        dma,
        dma,
        dma,
        dma,
        dma((Y,)),
        dma((Y,)),
        dma((ZH * ZL,)),
        dma((ZH * ZL,)),
        dma((X,)),
        dma((X,)),
        dma((Y,)),
        dma((Y,)),
        dma((Y,)),
        dma((Y,)),
    ]
    return pl.pallas_call(
        kernel,
        name="graph_layer",
        out_shape=(
            jax.ShapeDtypeStruct((T, T), bf16),
            jax.ShapeDtypeStruct((T, T), bf16),
            jax.ShapeDtypeStruct((T, T), f32),
        ),
        in_specs=[pl.BlockSpec(memory_space=pltpu.HBM)] * 6,
        out_specs=(vmem, vmem, vmem),
        scratch_shapes=scratch,
        compiler_params=pltpu.CompilerParams(
            collective_id=0, has_side_effects=True, vmem_limit_bytes=48 * 1024 * 1024
        ),
    )(
        *(
            pltpu.with_memory_space_constraint(v, pltpu.HBM)
            for v in (features, weight, upstream, adj, rows, live)
        )
    )


def solution(mesh):
    assert mesh.shape["blk"] == X * ZL and mesh.shape["rep"] == ZH * Y * 2
    in_specs = (
        P(("blk", "rep"), None),
        P(),
        P("blk", "rep", None, None, None, None, None),
        P("blk", "rep", None, None, None),
        P("blk", "rep", None, None),
        P(("blk", "rep"), None),
    )
    out_specs = (P(("blk", "rep"), None), P(("blk", "rep"), None), P())
    return jax.shard_map(local, mesh=mesh, in_specs=in_specs, out_specs=out_specs, check_vma=False)
```

```python
import functools

import jax
import jax.numpy as jnp
from jax import lax
from jax.experimental import pallas as pl
from jax.experimental.pallas import tpu as pltpu
from jax.sharding import PartitionSpec as P

MESH = pl.DeviceIdType.MESH
X, ZL, ZH, Y = 4, 8, 2, 4
ZQ = ZL // 2
T = 128


def dot(a, b):
    return jnp.dot(a, b, preferred_element_type=jnp.float32)


def kernel(
    feat_hbm,
    weight_hbm,
    up_hbm,
    adj_hbm,
    rows_hbm,
    live_hbm,
    hidden,
    input_grad,
    weight_grad,
    adj,
    up,
    up_far,
    weight,
    rows_v,
    live_v,
    tab_v,
    table,
    feats,
    sums,
    c1_out,
    c1_in,
    c2_out,
    c2_in,
    part,
    c3_out,
    c3_in,
    tops,
    slopes,
    terms,
    gx_out,
    gx_in,
    gz_out,
    gz_in,
    gz2_out,
    gz2_in,
    wg_out,
    h0_in,
    halves,
    h1_in,
    h2_buf,
    h3_buf,
    wg_all,
    ring_sem,
    in_sem,
    az_s,
    az_r,
    ax_s,
    ax_r,
    up_s,
    up_r,
    c1_s,
    c1_r,
    c2_s,
    c2_r,
    c3_s,
    c3_r,
    e2_s,
    e2_r,
    e3_s,
    e3_r,
    gx_s,
    gx_r,
    gz_s,
    gz_r,
    gz2_s,
    gz2_r,
    h0_s,
    h0_r,
    h1_s,
    h1_r,
    h2_s,
    h2_r,
    h3_s,
    h3_r,
    h4_s,
    h4_r,
    h5_s,
    h5_r,
):
    BLK, REP = X * ZL, ZH * Y * 2
    SL = 2 * BLK
    f32, bf16 = jnp.float32, jnp.bfloat16
    b = lax.axis_index("blk")
    r = lax.axis_index("rep")
    x, z = b // ZL, b % ZL
    zh, y, core = r // (2 * Y), (r // 2) % Y, r % 2
    ozh = (zh + 1) % ZH
    b_up, b_dn = (b + 1) % BLK, (b + BLK - 1) % BLK

    def at_z(d):
        return (x * ZL + (z + d) % ZL, r)

    def at_x(d):
        return (((x + d) % X) * ZL + z, r)

    def rep_of(h, v, c):
        return (h * Y + v) * 2 + c

    def at_y(d):
        return (b, rep_of(zh, (y + d) % Y, core))

    first, last = (ZL - z) // ZL, (z + 1) // ZL

    def at_dn(d):
        return (b_dn, rep_of((zh + first) % ZH, (y + d) % Y, core))

    def at_up(d):
        return (b_up, rep_of((zh + last) % ZH, (y + d) % Y, core))

    def at_ring(i):
        v = (zh * ZL + z + i) % (ZH * ZL)
        return (x * ZL + v % ZL, rep_of(v // ZL, y, core))

    sib = (b, rep_of(zh, y, 1 - core))
    r_oz = rep_of(ozh, y, core)

    def rc(src, dst, ss, rs, dev):
        return pltpu.make_async_remote_copy(
            src_ref=src, dst_ref=dst, send_sem=ss, recv_sem=rs, device_id=dev, device_id_type=MESH
        )

    in_copies = [
        pltpu.make_async_copy(src, dst, in_sem.at[i])
        for i, (src, dst) in enumerate(
            (
                (feat_hbm, feats.at[b]),
                (rows_hbm, rows_v),
                (live_hbm, live_v),
                (weight_hbm, weight),
                (adj_hbm, adj),
                (up_hbm, up),
            )
        )
    ]
    for copy in in_copies:
        copy.start()

    bar = pltpu.get_barrier_semaphore()

    def greet(dev):
        pl.semaphore_signal(bar, inc=1, device_id=dev, device_id_type=MESH)

    for i in range(ZQ, 0, -1):
        greet(at_ring(i))
        greet(at_ring(ZH * ZL - i))
    for d in range(1, X):
        greet(at_x(d))
    for d in range(1, Y):
        greet(at_y(d))
    greet(sib)
    for d in range(Y):
        greet(at_up(d))
        greet(at_dn(d))

    half, zq = z // ZQ, z % ZQ
    ohalf = 1 - half

    def other(m):
        v, bit = zq, 1
        while bit <= m:
            if m & bit:
                v = v + bit - 2 * bit * ((zq // bit) % 2)
            bit *= 2
        return v

    sums[2 * SL] = jnp.zeros((T, T), f32)
    slopes[2 * REP] = jnp.zeros((T, T), bf16)
    in_copies[0].wait()

    sends = []

    def go(copy):
        copy.start()
        sends.append(copy)
        return copy

    def flush(keep):
        done = sends[: len(sends) - keep]
        del sends[: len(done)]
        for copy in done:
            copy.wait_send()

    pl.semaphore_wait(bar, 2 * ZQ + (X - 1) + (Y - 1) + 1 + 2 * Y)

    def zsrc(g):
        return (half, ohalf)[g // ZQ] * ZQ + other(g % ZQ)

    def mate(m):
        return (x * ZL + half * ZQ + other(m), r)

    partner = (x * ZL + ohalf * ZQ + zq, r)

    def az_copy(g, v, dev):
        slot = feats.at[x * ZL + v]
        return rc(slot, slot, az_s.at[g], az_r.at[g], dev)

    def ax_copy(g, e, v):
        slot = feats.at[v * ZL + zsrc(g)]
        return rc(slot, slot, ax_s.at[e, g], ax_r.at[e, g], at_x(e))

    def along_x(g):
        for e in sorted(range(1, X), key=lambda e: min(e, X - e)):
            go(ax_copy(g, e, x))

    go(az_copy(ZQ, z, partner))
    for m in range(1, ZQ):
        go(az_copy(m, z, mate(m)))
    along_x(0)

    for i in (ZQ, ZH * ZL - ZQ):
        pl.semaphore_signal(ring_sem, inc=1, device_id=at_ring(i), device_id_type=MESH)

    in_copies[1].wait()
    in_copies[2].wait()
    i_s = lax.broadcasted_iota(jnp.int32, (BLK, BLK), 0)
    i_l = lax.broadcasted_iota(jnp.int32, (BLK, BLK), 1)

    def rank(n):
        far = ((n // ZQ) % 2) ^ half
        return (far * ZQ + (zq ^ (n % ZQ))) * X + ((x - n // ZL) & (X - 1))

    rank_s, rank_l = rank(i_s), rank(i_l)

    def to_rows(lanes):
        return jnp.sum(jnp.where(i_s == i_l, lanes, 0), axis=1, keepdims=True)

    t_l = lax.broadcasted_iota(jnp.int32, (BLK, REP), 1)
    for s in range(2):
        row_s = [to_rows(rows_v[s, k : k + 1, :]) for k in range(2)]
        live_l = live_v[s : s + 1, :]
        live_s = to_rows(live_l)
        code = [(2 * rank_s + k) * 1024 + s * SL + 2 * i_s + k for k in range(2)]

        def best(hits):
            found = jnp.max(jnp.maximum(hits[0], hits[1]), axis=0, keepdims=True)
            return jnp.where(found < 0, 2 * SL, found & 1023)

        for k in range(2):
            row_l = rows_v[s, k : k + 1, :]
            hits = [
                jnp.where(
                    (row_s[o] == row_l) & (live_s > o) & (2 * rank_s + o < 2 * rank_l + k),
                    code[o],
                    -1,
                )
                for o in range(2)
            ]
            tab_v[2 * s + k : 2 * s + k + 1, :BLK] = best(hits)
            spot = (((row_l & 1) * Y + ((row_l // 2) & (Y - 1))) * ZH + row_l // (2 * Y)) * 2 + s
            tab_v[6 + 2 * s + k : 7 + 2 * s + k, :BLK] = jnp.where(live_l > k, spot, 2 * REP)
        hits = [
            jnp.where((row_s[o] == t_l) & (live_s > o), code[o][:, :1], -1) for o in range(2)
        ]
        tab_v[4 + s : 5 + s, :REP] = best(hits)
    to_scalars = pltpu.make_async_copy(tab_v, table, in_sem.at[6])
    to_scalars.start()

    for m in range(1, ZQ):
        az_copy(m, zsrc(m), mate(m)).wait_recv()
        along_x(m)
    az_copy(ZQ, zsrc(ZQ), partner).wait_recv()
    for m in range(1, ZQ):
        go(az_copy(ZQ + m, zsrc(ZQ), mate(m)))
    along_x(ZQ)
    in_copies[4].wait()
    to_scalars.wait()


    def forward(g):
        for e in range(X):
            v = (x + X - e) % X
            if e:
                ax_copy(g, e, v).wait_recv()
            n = v * ZL + zsrc(g)
            for s in range(2):
                q = s * SL + 2 * n
                prod = dot(adj[pl.ds(q, 2)].reshape(2 * T, T), feats[n])
                sums[q] = prod[:T] + sums[table[2 * s, n]]
                sums[q + 1] = prod[T:] + sums[table[2 * s + 1, n]]

    early = ZQ // 2
    for g in range(early):
        forward(g)
    for m in range(1, ZQ):
        az_copy(ZQ + m, zsrc(ZQ + m), mate(m)).wait_recv()
        along_x(ZQ + m)
    for g in range(early, ZL):
        forward(g)

    def routed(s, t):
        return sums[table[4 + s, t]]

    def up_copy():
        return rc(up, up_far, up_s, up_r, (b, r_oz))

    in_copies[5].wait()
    pl.semaphore_wait(ring_sem, 2)
    go(up_copy())
    order = tuple(sorted(range(1, Y), key=lambda d: -min(d, Y - d))) + (0,)

    def c1_copy(h, d):
        return rc(c1_out.at[h, d], c1_in.at[h, d], c1_s.at[h, d], c1_r.at[h, d], sib)

    def c2_copy(h, s, d):
        dev = at_dn(d) if s else at_y(d)
        i = (h, s, d)
        return rc(c2_out.at[i], c2_in.at[i], c2_s.at[i], c2_r.at[i], dev)

    def c3_copy(h):
        return rc(c3_out.at[h], c3_in.at[h], c3_s.at[h], c3_r.at[h], (b, r_oz))

    for h in range(ZH):
        for d in order:
            for s in range(2):
                c1_out[h, d, s] = routed(s, rep_of(h, (y + d) % Y, 1 - core)).astype(bf16)
            go(c1_copy(h, d))
    for h in range(ZH):
        for d in order:
            c1_copy(h, d).wait_recv()
            for s in (1, 0):
                both = routed(s, rep_of(h, (y + d) % Y, core)) + c1_in[h, d, s].astype(f32)
                if s or d:
                    c2_out[h, s, d] = both.astype(bf16)
                    go(c2_copy(h, s, d))
                else:
                    part[h] = both
    for h in range(ZH):
        t = part[h]
        for s in range(2):
            for d in range(1 - s, Y):
                c2_copy(h, s, d).wait_recv()
                t = t + c2_in[h, s, d].astype(f32)
        part[h] = t
        c3_out[h] = t.astype(bf16)
        go(c3_copy(h))
    flush(ZH)
    up_copy().wait_recv()

    def place(s, h, v, c):
        return ((c * Y + v) * ZH + h) * 2 + s

    def tile(s, h, v, c):
        return slopes.at[place(s, h, v, c)]

    def e2_copy(h, s, d):
        dev = at_up(d) if s else at_y(d)
        own = tile(0, h, y, core)
        return rc(own, tile(s, h, y, core), e2_s.at[h, s, d], e2_r.at[h, s, d], dev)

    def e3_copy(h, d, c):
        both = slopes.at[pl.ds(place(0, h, (y + Y - d) % Y, c), 2)]
        return rc(both, both, e3_s.at[h, d], e3_r.at[h, d], sib)

    in_copies[3].wait()
    w = weight[...]
    for h in range(ZH):
        c3_copy(h).wait_recv()
        gathered = part[h] + c3_in[h].astype(f32)
        high = gathered.astype(bf16)
        low = (gathered - high.astype(f32)).astype(bf16)
        tops[h] = high
        summed = dot(high, w) + dot(low, w)
        sig = jax.nn.sigmoid(summed)
        given = jnp.where(zh == h, up[...], up_far[...]).astype(f32)
        slope = given * (sig * (1.0 + summed * (1.0 - sig)))
        slopes[place(0, h, y, core)] = slope.T.astype(bf16)
        for d in order:
            go(e2_copy(h, 1, d))
            if d:
                go(e2_copy(h, 0, d))
        part[h] = summed * sig
    hidden[...] = part[zh].astype(bf16)

    U = T // (2 * Y)
    total = dot(slopes[place(0, zh, y, core)], tops[zh])
    wg_out[...] = total.reshape(2 * Y, U, T)

    def h0_copy():
        return rc(wg_out.at[pl.ds((1 - core) * Y, Y)], h0_in, h0_s, h0_r, sib)

    go(h0_copy())

    def h1_copy(d):
        return rc(halves.at[(y + d) % Y], h1_in.at[d], h1_s.at[d], h1_r.at[d], at_y(d))

    h0_copy().wait_recv()
    halves[...] = wg_out[pl.ds(core * Y, Y)] + h0_in[...]
    for d in range(1, Y):
        go(h1_copy(d))

    def to_sibling(h):
        for d in (0,) + order[:-1]:
            for s in range(2):
                if s or d:
                    e2_copy(h, s, d).wait_recv()
            go(e3_copy(h, d, core))

    to_sibling(0)

    zz = zh * ZL + z

    def h2_copy(i, to):
        h, d = (zh + i // ZL) % ZH, i % ZL
        v = (z + (d if to else ZL - d)) % ZL
        slot = h2_buf.at[zz] if to else h2_buf.at[h * ZL + v]
        dev = (x * ZL + v, rep_of(h, y, core))
        return rc(slot, slot, h2_s.at[i], h2_r.at[i], dev)

    unit = halves[y]
    for d in range(1, Y):
        h1_copy(d).wait_recv()
        unit = unit + h1_in[d]
    h2_buf[zz] = unit.astype(bf16)
    for i in range(1, ZH * ZL):
        go(h2_copy(i, True))

    for h in range(1, ZH):
        to_sibling(h)

    for h in range(ZH):
        for d in range(Y):
            e3_copy(h, d, 1 - core).wait_recv()

    def backward(n):
        out = None
        for s in range(2):
            q = s * SL + 2 * n
            lhs = jnp.concatenate(
                [slopes[table[6 + 2 * s, n]], slopes[table[7 + 2 * s, n]]], axis=1
            )
            term = dot(lhs, adj[pl.ds(q, 2)].reshape(2 * T, T))
            out = term if out is None else out + term
        out = out.astype(bf16)
        terms[n] = out

    ZP = ZQ // 2
    turn_x, mirror_x = x + 1 - 2 * (x % 2), X - 1 - x
    over_x = (x + X // 2) % X
    meets = ((turn_x, mirror_x), (mirror_x, turn_x))

    def spot_of(v, k, g):
        return v * ZL + (ohalf, half)[k] * ZQ + g * ZP

    def gx_copy(k, g, step):
        to = (meets[g][step // 2] * ZL + z, r)
        i = (k, g, step)
        if step == 2:
            src = gx_out.at[k, g]
        else:
            src = terms.at[pl.ds(spot_of((over_x, meets[g][0])[step], k, g), ZP)]
        return rc(src, gx_in.at[i], gx_s.at[i], gx_r.at[i], to)

    def column_tiles(v, k):
        for g in range(2):
            for i in range(ZP):
                backward(spot_of(v[g], k, g) + i)

    def first_step(k, step):
        column_tiles(((over_x, over_x), (turn_x, mirror_x))[step], k)
        for g in range(2):
            go(gx_copy(k, g, step))

    def second_step(k):
        for g in range(2):
            gx_copy(k, g, 0).wait_recv()
            mine = terms[pl.ds(spot_of(meets[g][1], k, g), ZP)].astype(f32)
            gx_out[k, g] = (mine + gx_in[k, g, 0].astype(f32)).astype(bf16)
            go(gx_copy(k, g, 2))

    first_step(0, 0)
    first_step(0, 1)
    first_step(1, 0)
    for k in range(2):
        column_tiles((mirror_x, turn_x), k)
    second_step(0)
    first_step(1, 1)
    for k in range(2):
        column_tiles((x, x), k)
    second_step(1)

    def gx_sum(k, v):
        g, i = v // ZP, v % ZP
        t = terms[spot_of(x, k, 0) + v].astype(f32)
        return t + gx_in[k, g, 1, i].astype(f32) + gx_in[k, g, 2, i].astype(f32)

    def gz_copy(k, m):
        v = other(m)
        return rc(
            gz_out.at[k, m],
            gz_in.at[k, m],
            gz_s.at[k, m],
            gz_r.at[k, m],
            (x * ZL + half * ZQ + v, r),
        )

    def gx_wait(k):
        for g in range(2):
            for step in (1, 2):
                gx_copy(k, g, step).wait_recv()
        for m in range(1, ZQ):
            gz_out[k, m] = gx_sum(k, other(m)).astype(bf16)
            go(gz_copy(k, m))
        return gx_sum(k, zq)

    flush(12)
    crossing = gx_wait(0)

    def h3_copy(e, v):
        return rc(h3_buf.at[v], h3_buf.at[v], h3_s.at[e], h3_r.at[e], at_x(e))

    for i in range(1, ZH * ZL):
        h2_copy(i, False).wait_recv()
    unit = h2_buf[0].astype(f32)
    for i in range(1, ZH * ZL):
        unit = unit + h2_buf[i].astype(f32)
    h3_buf[x] = unit
    for e in range(1, X):
        go(h3_copy(e, x))

    kept = gx_wait(1)

    def h4_copy(d, v):
        slot = wg_all.at[core * Y + v]
        return rc(slot, slot, h4_s.at[d], h4_r.at[d], at_y(d))

    def h5_copy(d, c):
        slot = wg_all.at[c * Y + (y + Y - d) % Y]
        return rc(slot, slot, h5_s.at[d], h5_r.at[d], sib)

    for e in range(1, X):
        h3_copy(e, (x + X - e) % X).wait_recv()
    unit = h3_buf[0]
    for e in range(1, X):
        unit = unit + h3_buf[e]
    wg_all[core * Y + y] = unit
    for d in range(1, Y):
        go(h4_copy(d, y))
    go(h5_copy(0, core))

    def gz2_copy():
        return rc(gz2_out, gz2_in, gz2_s, gz2_r, (x * ZL + ohalf * ZQ + zq, r))

    for m in range(1, ZQ):
        gz_copy(0, m).wait_recv()
        crossing = crossing + gz_in[0, m].astype(f32)
    gz2_out[...] = crossing.astype(bf16)
    go(gz2_copy())
    for m in range(1, ZQ):
        gz_copy(1, m).wait_recv()
        kept = kept + gz_in[1, m].astype(f32)

    flush(1)
    for d in range(1, Y):
        h4_copy(d, (y + Y - d) % Y).wait_recv()
        go(h5_copy(d, core))

    for d in range(Y):
        h5_copy(d, 1 - core).wait_recv()
    weight_grad[...] = wg_all[...].reshape(T, T).T

    gz2_copy().wait_recv()
    pulled = (kept + gz2_in[...].astype(f32)).T.astype(bf16)
    input_grad[...] = lax.dot_general(
        pulled, w, (((1,), (1,)), ((), ())), preferred_element_type=f32
    ).astype(bf16)

    flush(0)


def local(features, weight, adjacency, row_tiles, live_counts, upstream):
    BLK, REP = X * ZL, ZH * Y * 2
    f32, bf16 = jnp.float32, jnp.bfloat16
    adj = adjacency.reshape(4 * BLK, T, T)
    rows = jnp.swapaxes(row_tiles, 3, 4).reshape(2, 2, BLK)
    live = live_counts.reshape(2, BLK)
    vmem = pl.BlockSpec(memory_space=pltpu.VMEM)

    def buf(*dims, dtype=bf16):
        return pltpu.VMEM(dims + (T,), dtype)

    U = T // (2 * Y)
    dma = pltpu.SemaphoreType.DMA
    scratch = [
        buf(4 * BLK, T),
        buf(T),
        buf(T),
        buf(T),
        pltpu.VMEM((2, 2, BLK), jnp.int32),
        pltpu.VMEM((2, BLK), jnp.int32),
        buf(16, dtype=jnp.int32),
        pltpu.SMEM((16, T), jnp.int32),
        buf(BLK, T),
        buf(4 * BLK + 1, T, dtype=f32),
        buf(ZH, Y, 2, T),
        buf(ZH, Y, 2, T),
        buf(ZH, 2, Y, T),
        buf(ZH, 2, Y, T),
        buf(ZH, T, dtype=f32),
        buf(ZH, T),
        buf(ZH, T),
        buf(ZH, T),
        buf(2 * REP + 1, T),
        buf(BLK, T),
        buf(2, 2, ZQ // 2, T),
        buf(2, 2, 3, ZQ // 2, T),
        buf(2, ZQ, T),
        buf(2, ZQ, T),
        buf(T),
        buf(T),
        buf(2 * Y, U, dtype=f32),
        buf(Y, U, dtype=f32),
        buf(Y, U, dtype=f32),
        buf(Y, U, dtype=f32),
        buf(ZH * ZL, U),
        buf(X, U, dtype=f32),
        buf(2 * Y, U, dtype=f32),
        pltpu.SemaphoreType.REGULAR,
        dma((7,)),
        dma((ZL,)),
        dma((ZL,)),
        dma((X, ZL)),
        dma((X, ZL)),
        dma,
        dma,
        dma((ZH, Y)),
        dma((ZH, Y)),
        dma((ZH, 2, Y)),
        dma((ZH, 2, Y)),
        dma((ZH,)),
        dma((ZH,)),
        dma((ZH, 2, Y)),
        dma((ZH, 2, Y)),
        dma((ZH, Y)),
        dma((ZH, Y)),
        dma((2, 2, 3)),
        dma((2, 2, 3)),
        dma((2, ZQ)),
        dma((2, ZQ)),
        dma,
        dma,
        dma,
        dma,
        dma((Y,)),
        dma((Y,)),
        dma((ZH * ZL,)),
        dma((ZH * ZL,)),
        dma((X,)),
        dma((X,)),
        dma((Y,)),
        dma((Y,)),
        dma((Y,)),
        dma((Y,)),
    ]
    return pl.pallas_call(
        kernel,
        name="graph_layer",
        out_shape=(
            jax.ShapeDtypeStruct((T, T), bf16),
            jax.ShapeDtypeStruct((T, T), bf16),
            jax.ShapeDtypeStruct((T, T), f32),
        ),
        in_specs=[pl.BlockSpec(memory_space=pltpu.HBM)] * 6,
        out_specs=(vmem, vmem, vmem),
        scratch_shapes=scratch,
        compiler_params=pltpu.CompilerParams(
            collective_id=0, has_side_effects=True, vmem_limit_bytes=48 * 1024 * 1024
        ),
    )(
        *(
            pltpu.with_memory_space_constraint(v, pltpu.HBM)
            for v in (features, weight, upstream, adj, rows, live)
        )
    )


def solution(mesh):
    assert mesh.shape["blk"] == X * ZL and mesh.shape["rep"] == ZH * Y * 2
    in_specs = (
        P(("blk", "rep"), None),
        P(),
        P("blk", "rep", None, None, None, None, None),
        P("blk", "rep", None, None, None),
        P("blk", "rep", None, None),
        P(("blk", "rep"), None),
    )
    out_specs = (P(("blk", "rep"), None), P(("blk", "rep"), None), P())
    return jax.shard_map(local, mesh=mesh, in_specs=in_specs, out_specs=out_specs, check_vma=False)
```
